256 devices in a mesh: leaf: 64 (over x, z, core), rhs: 4 (over y).
Axes of the slice: x: 4, y: 4, z: 8, core: 2. Of those that a mesh axis runs over, the one named last changes fastest.
Arguments:
- coords: float32 [2, 1048576], P(None, 'leaf'), may hold values from 0 to 1
- charges: float32 [8, 1048576], P('rhs', 'leaf'), may hold values from -6 to 6
- leaf_basis: float32 [1024, 64, 1024], P('leaf'), may hold values from -0.1875 to 0.1875
- transfer: float32 [128, 15, 64, 64], P('leaf'), may hold values from -0.75 to 0.75
- coupling: float32 [128, 124, 64, 64], P('leaf'), may hold values from -0.25 to 0.25
- far_pairs: int32 [128, 124], P('leaf'), may hold values from 0 to 1023, as said below
- near_list: int32 [1024, 9], P('leaf'), may hold values from 0 to 1023, as said below
- near_count: int32 [1024], P('leaf'), may hold values from 1 to 9, as said below
Outputs:
- potential: float32 [8, 1048576], P('rhs', 'leaf')
The draws below stay inside these ranges and needn't reach their ends.
Inputs may be any that keep to these rules, and one draw needn't show every extreme that they name: `near_list`: row i names the leaves that act on leaf i directly: its first entry is i, its first near_count[i] entries are distinct, the rest repeat i. Every named leaf j lies at most one strip row and one column from i, so |j - i| <= 5; j names i whenever i names j. `near_count`: the number of live entries of the matching row of near_list. `far_pairs`: each entry names a cluster of its pair's level other than the pair's target.
All inputs are finite; a program needn't handle non-finite values.
Results may differ from the reference program's by a relative error of at most 0.0003.
Values sent between devices are 32-bit elements; how exact they have to be, the bound alone decides.
No kernel may reach another device: no remote copies, remote signals or barrier semaphores. Data moves between devices by JAX's collectives and lax.ppermute only.
A program may use at most 128 MiB of HBM per device.

```python
import jax
import jax.numpy as jnp
import numpy as np
from jax import lax

PTS = 1024
RANK = 64
NRHS = 8
NEAR = 9
FAR = 8
STRIP = 4
LEAF_DEV = 16
NLEAF = 1024
NPTS = 1048576
NBLK = 128
PSLOTS = 124


FORWARD_STEPS = ((0, 1), (1, -1), (1, 0), (1, 1))


def near_pattern(key):
    leaf_ids = jnp.arange(NLEAF, dtype=jnp.int32)
    strip_row = leaf_ids // STRIP
    strip_col = leaf_ids % STRIP
    row_total = NLEAF // STRIP
    key_group, key_bits, random_key_row, key_col = jax.random.split(key, 4)
    region = jax.random.randint(key_group, (NLEAF // LEAF_DEV,), 0, 2)
    cutoff = 4 + 3 * jnp.repeat(region, LEAF_DEV)
    coins = jax.random.randint(key_bits, (NLEAF, 4), 0, 8) < cutoff[:, None]
    forced = jax.random.randint(random_key_row, (), 1, row_total - 1) * STRIP + jax.random.randint(key_col, (), 1, STRIP - 1)
    partners = [leaf_ids]
    valids = [jnp.ones((NLEAF,), jnp.bool_)]
    for step_index in range(4):
        move_row, move_col = FORWARD_STEPS[step_index]
        for direction in (1, -1):
            updated_row = strip_row + direction * move_row
            new_col = strip_col + direction * move_col
            inside = (updated_row >= 0) & (updated_row < row_total) & (new_col >= 0) & (new_col < STRIP)
            other = jnp.where(inside, updated_row * STRIP + new_col, leaf_ids)
            lower = leaf_ids if direction == 1 else other
            coin = coins[lower, step_index]
            live = inside & (coin | (leaf_ids == forced) | (other == forced))
            partners.append(jnp.where(live, other, leaf_ids))
            valids.append(live)
    partner_table = jnp.stack(partners, axis=1)
    valid_table = jnp.stack(valids, axis=1)
    sort_key = jnp.where(valid_table, 0, 16) + jnp.arange(NEAR, dtype=jnp.int32)[None, :]
    order = jnp.argsort(sort_key, axis=1, stable=True)
    near_table = jnp.take_along_axis(partner_table, order, axis=1).astype(jnp.int32)
    live_count = jnp.sum(valid_table.astype(jnp.int32), axis=1).astype(jnp.int32)
    return (near_table, live_count)


def draw_near_list(key, part):
    pattern = near_pattern(key)
    return pattern[0]


def draw_near_count(key, part):
    pattern = near_pattern(key)
    return pattern[1]


def draw_far_pairs(key, part):
    key = jax.random.fold_in(key, 23)
    sizes_np = [8 * FAR // 2 ** height for height in range(5)]
    within_np = np.concatenate([np.arange(size_here) for size_here in sizes_np])
    per_block_np = np.concatenate([np.full(size_here, size_here) for size_here in sizes_np])
    clusters_np = np.concatenate([np.full(sizes_np[height], NLEAF // 2 ** height) for height in range(5)])
    block_ids = jnp.arange(NBLK, dtype=jnp.int32)[:, None]
    pair_index = block_ids * jnp.asarray(per_block_np, jnp.int32)[None, :] + jnp.asarray(within_np, jnp.int32)[None, :]
    target = pair_index // FAR
    cluster_count = jnp.asarray(clusters_np, jnp.int32)[None, :]
    raw = jax.random.randint(key, (NBLK, PSLOTS), 0, cluster_count - 1)
    result = (raw + (raw >= target).astype(jnp.int32)).astype(jnp.int32)
    result = result.at[0, 0].set(NLEAF - 1)
    result = result.at[NBLK - 1, 0].set(0)
    return result.astype(jnp.int32)


def block_scale(stream_key, dims, cuts, least, top_value):
    factor_of, own = 1.0, jax.random.fold_in(stream_key, 6)
    for dim, blocks in cuts:
        steps = jnp.exp(jax.random.uniform(jax.random.fold_in(own, dim), (blocks,), jnp.float32, least / len(cuts), top_value / len(cuts)))
        factor_of = factor_of * jnp.repeat(steps, dims[dim] // blocks).reshape([-1 if axis == dim else 1 for axis in range(len(dims))])
    return factor_of


def normal_values(stream_key, extent, deviation, bound, pieces=(), kind=jnp.bfloat16):
    values = jax.random.normal(stream_key, extent, jnp.float32) * deviation
    if len(pieces) > 0:
        values = block_scale(stream_key, extent, pieces, -0.22, 0.18) * values
    return jnp.clip(values, min=-bound, max=bound).astype(kind)


def setup_inputs(seed: int = 0) -> dict:
    key_list = jax.random.split(jax.random.key(seed), 9)
    coords = jnp.clip(1.0 * jax.random.uniform(key_list[0], (2, NPTS), jnp.float32) ** block_scale(key_list[0], (2, NPTS), ((1, 64),), -0.2, 0.2), 0.0, 1.0)
    charges = normal_values(key_list[1], (NRHS, NPTS), 1.0, 6.0, ((0, 4), (1, 64)), jnp.float32)
    leaf_basis = normal_values(key_list[2], (NLEAF, RANK, PTS), PTS ** -0.5, 0.1875, ((0, 64),), jnp.float32)
    transfer = normal_values(key_list[3], (NBLK, 15, RANK, RANK), RANK ** -0.5, 0.75, ((0, 64),), jnp.float32)
    coupling = normal_values(key_list[4], (NBLK, PSLOTS, RANK, RANK), (RANK * FAR) ** -0.5, 0.25, ((0, 64),), jnp.float32)
    far_pairs = draw_far_pairs(jax.random.fold_in(key_list[8], 71), 0)
    near_list = draw_near_list(jax.random.fold_in(key_list[8], 71), 0)
    near_count = draw_near_count(jax.random.fold_in(key_list[8], 71), 0)
    return {"coords": coords, "charges": charges, "leaf_basis": leaf_basis, "transfer": transfer, "coupling": coupling, "far_pairs": far_pairs, "near_list": near_list, "near_count": near_count}


TOP_PRECISION = lax.Precision.HIGHEST
TRANSFER_OFFSETS = (0, 8, 12, 14)
DECAY_RATE = 4.0

def near_leaf(leaf_id, coord_leaf, charge_leaf, near_list, near_count):
    own = coord_leaf[:, leaf_id]
    target_row = own[0] + (leaf_id // STRIP).astype(jnp.float32)
    target_col = own[1] + (leaf_id % STRIP).astype(jnp.float32)

    def add_slot(running, slot_index):
        partner = near_list[leaf_id, slot_index]
        source = coord_leaf[:, partner]
        source_row = source[0] + (partner // STRIP).astype(jnp.float32)
        source_col = source[1] + (partner % STRIP).astype(jnp.float32)
        distance = jnp.sqrt((target_row[:, None] - source_row[None, :]) ** 2 + (target_col[:, None] - source_col[None, :]) ** 2)
        weight = jnp.where(slot_index < near_count[leaf_id], PTS ** (-0.5), 0.0)
        kernel = jnp.exp(-DECAY_RATE * distance) * weight
        return (running + jnp.dot(charge_leaf[:, partner], kernel.T, precision=TOP_PRECISION), None)
    running, _ = lax.scan(add_slot, jnp.zeros((NRHS, PTS), jnp.float32), jnp.arange(NEAR, dtype=jnp.int32))
    return running

def reference(coords, charges, leaf_basis, transfer, coupling, far_pairs, near_list, near_count):
    coord_leaf = coords.reshape(2, NLEAF, PTS)
    charge_leaf = charges.reshape(NRHS, NLEAF, PTS)
    near_all = lax.map(lambda leaf_id: near_leaf(leaf_id, coord_leaf, charge_leaf, near_list, near_count), jnp.arange(NLEAF, dtype=jnp.int32))
    near_part = jnp.transpose(near_all, (1, 0, 2))
    skeleton = jnp.einsum('arp,cap->acr', leaf_basis, charge_leaf, precision=TOP_PRECISION)
    levels_up = [skeleton]
    transfer_sets = []
    current = skeleton
    for height in range(1, 5):
        slot_count = 8 // 2 ** (height - 1)
        start = TRANSFER_OFFSETS[height - 1]
        transfer_block = transfer[:, start:start + slot_count].reshape(-1, RANK, RANK)
        transfer_sets.append(transfer_block)
        lifted = jnp.einsum('ncr,nrq->ncq', current, transfer_block, precision=TOP_PRECISION)
        current = lifted.reshape(-1, 2, NRHS, RANK).sum(1)
        levels_up.append(current)
    targets = []
    offset = 0
    for height in range(5):
        slot_count = 8 * FAR // 2 ** height
        local_blocks = coupling[:, offset:offset + slot_count].reshape(-1, RANK, RANK)
        sources = far_pairs[:, offset:offset + slot_count].reshape(-1)
        selected = jnp.take(levels_up[height], sources, axis=0)
        matvec_output = jnp.einsum('vde,vte->vdt', selected, local_blocks, precision=TOP_PRECISION)
        targets.append(matvec_output.reshape(-1, FAR, NRHS, RANK).sum(1))
        offset = offset + slot_count
    downward = targets[4]
    for height in range(4, 0, -1):
        parent = jnp.repeat(downward, 2, axis=0)
        downward = targets[height - 1] + jnp.einsum('ncs,nrs->ncr', parent, transfer_sets[height - 1], precision=TOP_PRECISION)
    distant_portion = jnp.einsum('arp,acr->cap', leaf_basis, downward, precision=TOP_PRECISION)
    return (distant_portion + near_part).reshape(NRHS, NPTS)
```

```python
import functools

import jax
import jax.numpy as jnp
from jax import lax
from jax.experimental import pallas as pl
from jax.experimental.pallas import tpu as pltpu
from jax.sharding import PartitionSpec as P

F = jnp.float32
B = jnp.bfloat16
NN = (((1,), (0,)), ((), ()))
NT = (((1,), (1,)), ((), ()))
HI = lax.Precision.HIGHEST

FAR = 8
STRIP = 4
LEAVES = 16
PTS = 1024
QUART = 256
RANK = 64
NEAR = 9
RHS = 4
NX, NZ, NC = 4, 8, 2
LEVEL_ROW = (0, 16, 24, 28, 30)
TRANSFER_OFFSETS = (0, 8, 12, 14)
RATE = -4.0 * 1.4426950408889634
S_LIMB = (0, 0, 1, 1, 0, 2, 1, 2)
T_LIMB = (0, 1, 0, 1, 2, 0, 2, 1)
PAIRS = 124
WINDOWS = 6
OVER = 152
ANY = pl.BlockSpec(memory_space=pl.ANY)
HBM = pl.BlockSpec(memory_space=pltpu.HBM)
VMEM = pl.BlockSpec(memory_space=pltpu.VMEM)
SMEM = pl.BlockSpec(memory_space=pltpu.SMEM)
PARAMS = pltpu.CompilerParams(vmem_limit_bytes=48 * 2**20)


def dot(a, b, dims):
    return lax.dot_general(a, b, dims, preferred_element_type=F)


def dot_hi(a, b, dims):
    return lax.dot_general(a, b, dims, preferred_element_type=F, precision=HI)


def call(kernel, outs, in_specs, scratch=(), micros=1.0, smem_outs=0):
    outs = [v if isinstance(v, jax.ShapeDtypeStruct) else jax.ShapeDtypeStruct(v, F) for v in outs]
    return pl.pallas_call(
        kernel,
        out_shape=outs,
        in_specs=in_specs,
        out_specs=[SMEM if n < smem_outs else VMEM for n in range(len(outs))],
        scratch_shapes=list(scratch),
        compiler_params=PARAMS,
        cost_estimate=pl.CostEstimate(
            flops=int(micros * 10**9), bytes_accessed=10**5, transcendentals=0
        ),
    )


def pre_kernel(meta, coords_hbm, charges_hbm, own, first, second, place, coords, charges, sems):
    copies = [
        pltpu.make_async_copy(charges_hbm, charges, sems.at[0]),
        pltpu.make_async_copy(coords_hbm, coords, sems.at[1]),
    ]
    for copy in copies:
        copy.start()
    r = meta[1]
    copies[0].wait()
    for k, (ref, at) in enumerate(((own, 0), (first, 0), (second, 0), (first, 2))):
        q = (r ^ k) * QUART
        for i in range(LEAVES):
            source = pl.ds(pl.multiple_of(q + i * PTS, QUART), QUART)
            ref[at : at + 2, i * QUART : (i + 1) * QUART] = charges[:, source]
    copies[1].wait()
    for i in range(LEAVES):
        source = pl.ds(pl.multiple_of(r * QUART + i * PTS, QUART), QUART)
        place[:, i * QUART : (i + 1) * QUART] = coords[:, source]


def limbs(v):
    first = v.astype(B).astype(F)
    rest = v - first
    second = rest.astype(B).astype(F)
    return first, second, rest - second


def pick(row, values, rest):
    out = rest
    for n, v in reversed(list(enumerate(values))):
        out = jnp.where(row == n, v, out)
    return out


def source_rows(x, y):
    shape = (8, x.shape[1])
    row = lax.broadcasted_iota(jnp.int32, shape, 0)
    x, y = jnp.broadcast_to(x, shape), jnp.broadcast_to(y, shape)
    lx, ly, ls = limbs(-2.0 * x), limbs(-2.0 * y), limbs(x * x + y * y)
    zero = jnp.zeros(shape, F)
    one = zero + 1.0
    return jnp.concatenate(
        [
            pick(row, [lx[a] for a in S_LIMB], zero),
            pick(row, [ly[a] for a in S_LIMB], zero),
            pick(row, [one, one, one, *ls], zero),
            pick(row, [*lx, *ly], zero),
        ],
        axis=0,
    )


def target_rows(x, y):
    shape = (8, x.shape[1])
    row = lax.broadcasted_iota(jnp.int32, shape, 0)
    lx, ly = (limbs(jnp.broadcast_to(v, shape)) for v in (x, y))
    zero = jnp.zeros(shape, F)
    return jnp.concatenate(
        [pick(row, [lx[b] for b in T_LIMB], zero), pick(row, [ly[b] for b in T_LIMB], zero)], axis=0
    ).astype(B)


def prep_kernel(meta, list_hbm, count_hbm, coords, place, _, lists, sf, tab, near_list, near_count, sems):
    copies = [
        pltpu.make_async_copy(list_hbm, near_list, sems.at[0]),
        pltpu.make_async_copy(count_hbm, near_count, sems.at[1]),
    ]
    for copy in copies:
        copy.start()
    for n in range(4):
        xy = place[:, 4 * n * QUART : 4 * (n + 1) * QUART] - 0.5
        put_sources(xy, sf, 4 * n)
    for i in range(LEAVES):
        xy = coords[:, i * PTS : (i + 1) * PTS] - 0.5
        tab[i] = target_rows(xy[0:1], xy[1:2])
    for copy in copies:
        copy.wait()
    first = meta[0]

    def leaf_pairs(i, counts):
        def slot(s, counts):
            local = near_list[i, s] - first
            before, after = local < 0, local >= LEAVES
            over = (before | after).astype(jnp.int32)
            p = jnp.where(over == 1, OVER + counts[1], counts[0])
            lists[0, p] = i
            lists[1, p] = jnp.where(before, local + 20, jnp.where(after, local + 4, local))
            lists[2, p] = i
            lists[3, p] = lax.shift_right_arithmetic(local, 2) - lax.shift_right_arithmetic(i, 2)
            lists[4, p] = (local & 3) - (i & 3)
            return counts[0] + 1 - over, counts[1] + over

        return lax.fori_loop(0, near_count[i], slot, counts)

    inside, over = lax.fori_loop(0, LEAVES, leaf_pairs, (jnp.int32(0), jnp.int32(0)))
    lists[5, 0] = inside
    lists[5, 1] = over
    for p in range(4):
        for field in range(5):
            lists[field, OVER + over + p] = LEAVES if field == 2 else 0


def put_sources(xy, sf, at):
    rows = source_rows(xy[0:1], xy[1:2])
    rows = jnp.concatenate([rows[:, n * QUART : (n + 1) * QUART] for n in range(4)], axis=0)
    turned = rows.T
    for n in range(4):
        sf[at + n] = turned[:, n * 32 : (n + 1) * 32].astype(B)


def weights(c):
    high = c.astype(B).astype(F)
    return jnp.concatenate([high, c - high], axis=0).astype(B)


def near_kernel(w, n_carried, *refs):
    refs = list(refs)

    def take(n):
        taken = refs[:n]
        del refs[:n]
        return taken

    last = w == WINDOWS - 1
    lists, coords, tab, sf = take(4)
    if w == 0:
        own, first, second, place = take(4)
    else:
        cw, acc_in = take(2)
    if w >= 4:
        halos = take(2)
    carried = take(n_carried)
    outs = take(4 if last else 1)
    if w == 0:
        cw, to_before, to_after = take(3)
    for ref, out in zip(carried, take(n_carried)):
        out[...] = ref[...]
    kh_a, kl_a, kh_b, kl_b = take(4)
    acc = take(1)[0] if last else outs[0]

    if w == 0:
        whole = jnp.concatenate([own[...], first[...], second[...]], axis=0)
        whole = jnp.concatenate([whole[0:4], whole[6:10]], axis=0)
        for j in range(LEAVES):
            cw[j] = weights(whole[:, j * QUART : (j + 1) * QUART])
        for ref, at in ((to_before, slice(0, 4 * QUART)), (to_after, slice(12 * QUART, 16 * QUART))):
            ref[0:2] = place[:, at]
            ref[2:10] = whole[:, at]
        acc[...] = jnp.zeros_like(acc)
    else:
        acc[...] = acc_in[...]
    if w >= 4:
        sf_own, cw_own = sf, cw
        sf, cw = take(2)
        sf[0:LEAVES] = sf_own[...]
        cw[0:LEAVES] = cw_own[...]
        for n, halo in enumerate(halos):
            put_sources(halo[0:2] - 0.5, sf, LEAVES + 4 * n)
            for j in range(4):
                cw[LEAVES + 4 * n + j] = weights(halo[2:10, j * QUART : (j + 1) * QUART])
    kh_b[...] = jnp.zeros_like(kh_b)
    kl_b[...] = jnp.zeros_like(kl_b)

    inside = lists[5, 0]
    total = inside + lists[5, 1]

    def bound(n):
        if n == 0:
            return jnp.int32(0)
        if n == WINDOWS:
            return total
        at = lax.div(total * n, WINDOWS)
        return (jnp.minimum(at, inside) if n <= 4 else at) & -2

    begin, end = bound(w), bound(w + 1)

    def entry(p):
        return jnp.where(p < inside, p, p - inside + OVER)

    row = lax.broadcasted_iota(jnp.int32, (8, PTS), 0)
    low, middle = row < 3, (row >= 3) & (row < 6)
    ones = jnp.where(middle, 1.0, 0.0)

    def evaluate(p, kh, kl):
        p = entry(p)
        i, j = lists[0, p], lists[1, p]
        ox, oy = lists[3, p].astype(F), lists[4, p].astype(F)
        xy = coords[:, pl.ds(pl.multiple_of(i * PTS, PTS), PTS)] - 0.5
        x = jnp.broadcast_to(xy[0:1], (8, PTS)) - ox
        y = jnp.broadcast_to(xy[1:2], (8, PTS)) - oy
        ls = limbs(x * x + y * y)
        squares = pick(row, ls, ones)
        offsets = jnp.where(low, -ox, jnp.where(middle, -oy, 0.0))
        t_rows = jnp.concatenate(
            [tab[i], jnp.concatenate([squares, offsets], axis=0).astype(B)], axis=0
        )
        s_rows = sf[j]
        for c in range(4):
            lanes = slice(c * 256, (c + 1) * 256)
            dist2 = dot(s_rows, t_rows[:, lanes], NN)
            for g in range(16):
                at = slice(g * 16, (g + 1) * 16)
                d2 = jnp.maximum(dist2[at], 1e-35)
                k = jnp.exp2((d2 * lax.rsqrt(d2)) * RATE)
                high = k.astype(B)
                kh[at, lanes] = high
                kl[at, lanes] = (k - high.astype(F)).astype(B)

    def multiply(p, kh, kl):
        p = entry(p)
        c = cw[lists[1, p]]
        acc[lists[2, p]] += dot(c, kh[...], NN) + dot(c, kl[...], NN)

    def step(n, _):
        p = begin + 2 * n
        evaluate(p, kh_a, kl_a)
        multiply(jnp.maximum(p - 1, 0), kh_b, kl_b)
        evaluate(p + 1, kh_b, kl_b)
        multiply(p, kh_a, kl_a)
        return 0

    steps = (end - begin + 1) // 2
    lax.fori_loop(0, steps, step, 0)
    multiply(jnp.maximum(begin + 2 * steps - 1, 0), kh_b, kl_b)

    if last:
        for i in range(LEAVES):
            v = (acc[i, 0:8, :] + acc[i, 8:16, :]) * (PTS**-0.5)
            for k in range(RHS):
                outs[k][:, i * PTS : (i + 1) * PTS] = v[2 * k : 2 * k + 2]


def bf16(*shape):
    return jax.ShapeDtypeStruct(shape, B)


def split_rows(v):
    high = v.astype(B).astype(F)
    return jnp.concatenate([high, v - high], axis=0).astype(B)


def split_dot(rows, matrix, dims):
    high = matrix.astype(B)
    low = (matrix - high.astype(F)).astype(B)
    v = dot(rows, high, dims) + dot(rows, low, dims)
    return v[0:8] + v[8:16]


def up_kernel(charges, basis, transfer, _, out):
    row = lax.broadcasted_iota(jnp.int32, (8, PTS), 0)

    def put(at, v):
        out[at : at + 1, 0:RANK] = v[0:1]
        out[at : at + 1, RANK : 2 * RANK] = v[1:2]

    current = []
    for i in range(LEAVES):
        c = charges[:, i * PTS : (i + 1) * PTS]
        c = jnp.where(row == 0, c[0:1], jnp.where(row == 1, c[1:2], 0.0))
        v = split_dot(split_rows(c), basis[i], NT)
        put(i, v)
        current.append(v)
    for level in range(1, 5):
        per_block = 8 >> (level - 1)
        lifted = [
            dot_hi(v, transfer[d // per_block, TRANSFER_OFFSETS[level - 1] + d % per_block], NN)
            for d, v in enumerate(current)
        ]
        current = [lifted[d] + lifted[d + 1] for d in range(0, len(lifted), 2)]
        for d, v in enumerate(current):
            put(LEVEL_ROW[level] + d, v)
    out[31:32, :] = jnp.zeros((1, 2 * RANK), F)


def couple(block, rows, table, coupling, picked, products):
    picked[120:128, :] = jnp.zeros((8, 2 * RANK), F)
    for q in range(PAIRS):
        picked[q : q + 1, :] = table[pl.ds(rows[block, q], 1), :]
    turned = picked[...].T
    g = [turned[c * RANK : (c + 1) * RANK, 0:PAIRS] for c in range(2)]

    def part(n, _):
        at = pl.ds(pl.multiple_of(n * 8, 8), 8)
        b = coupling[block, at]
        for c in range(2):
            products[c, at, :] = jnp.sum(b * g[c][None], axis=1)
        return 0

    lax.fori_loop(0, RANK // 8, part, 0)
    pair = lax.broadcasted_iota(jnp.int32, (16, PAIRS), 1)
    target = lax.broadcasted_iota(jnp.int32, (16, PAIRS), 0)
    member = jnp.where(lax.shift_right_arithmetic(pair, 3) == target, 1.0, 0.0)
    return [dot_hi(member, products[c], NT) for c in range(2)]


def first_kernel(rows, own, other, coupling, carried, table, out, carry, picked, products):
    half = own.shape[0]
    table[0:half, :] = own[...]
    table[half : 2 * half, :] = other[...]
    carry[...] = carried[...]
    for c, t in enumerate(couple(0, rows, table, coupling, picked, products)):
        out[c] = t


def second_kernel(rows, table, coupling, start, transfer, carried, out, carry, picked, products, held):
    carry[...] = carried[...]
    held[...] = jnp.zeros_like(held)
    for c, t in enumerate(couple(1, rows, table, coupling, picked, products)):
        for n in range(16):
            held[n, c : c + 1, :] = start[c, n : n + 1, :]
            held[16 + n, c : c + 1, :] = t[n : n + 1]
    current = [held[15] + held[31]]
    first = (0, 8, 12, 14)
    for level in range(4, 0, -1):
        per_block = 8 >> (level - 1)
        current = [
            held[16 * (d // per_block) + first[level - 1] + d % per_block]
            + dot_hi(
                current[d // 2],
                transfer[d // per_block, TRANSFER_OFFSETS[level - 1] + d % per_block],
                NT,
            )
            for d in range(2 * per_block)
        ]
    for i in range(LEAVES):
        out[i] = current[i]


def expand_kernel(coefficients, basis, _, out):
    for i in range(LEAVES):
        v = split_dot(split_rows(coefficients[i]), basis[i], NN)
        out[:, i * PTS : (i + 1) * PTS] = v[0:2]


def shards(coords, charges, leaf_basis, transfer, coupling, far_pairs, near_list, near_count):
    device = lax.axis_index("leaf").astype(jnp.int32)
    rhs_index = lax.axis_index("rhs").astype(jnp.int32)
    meta = jnp.stack([device * LEAVES, rhs_index])
    count = NX * NZ * NC

    def swap_rhs(v, k):
        return lax.ppermute(v, "rhs", [(i, i ^ k) for i in range(RHS)])

    def swap_leaf(v, bit):
        return lax.ppermute(v, "leaf", [(d, d ^ bit) for d in range(count)])

    own, first, second, place = call(
        pre_kernel,
        [(2, LEAVES * QUART), (4, LEAVES * QUART), (2, LEAVES * QUART), (2, LEAVES * QUART)],
        [SMEM, HBM, HBM],
        [
            pltpu.VMEM((2, LEAVES * PTS), F),
            pltpu.VMEM((2, LEAVES * PTS), F),
            pltpu.SemaphoreType.DMA((2,)),
        ],
    )(meta, coords, charges)
    first = swap_rhs(first, 1)
    lists, sf, tab = call(
        prep_kernel,
        [jax.ShapeDtypeStruct((6, 320), jnp.int32), bf16(LEAVES, QUART, 32), bf16(LEAVES, 16, PTS)],
        [SMEM, HBM, HBM, VMEM, VMEM, ANY],
        [
            pltpu.SMEM((LEAVES, NEAR), jnp.int32),
            pltpu.SMEM((LEAVES,), jnp.int32),
            pltpu.SemaphoreType.DMA((2,)),
        ],
        micros=4,
        smem_outs=1,
    )(meta, near_list, near_count, coords, place, own)
    onward = jnp.concatenate([second, first[2:4]], 0)
    second = swap_rhs(onward, 2)
    (table,) = call(up_kernel, [(32, 2 * RANK)], [VMEM] * 3 + [ANY], micros=4)(
        charges, leaf_basis, transfer, onward
    )

    acc_shape, halo_shape = (LEAVES + 1, 16, PTS), (10, 4 * QUART)
    values = [pltpu.VMEM((QUART, PTS), B)] * 4
    after = table
    halos = []
    for w, bit in enumerate((2, 4, 8, 16, 32, 1)):
        swapped = swap_leaf(after, bit)
        carried = [after] if w < WINDOWS - 1 else []
        data, extra, scratch = [lists, coords, tab, sf], [], [*values]
        if w == 0:
            data += [own, first, second, place]
            extra = [bf16(LEAVES, 16, QUART), halo_shape, halo_shape]
        else:
            data += [cw, acc]
        if w == 1:
            carried.append(to_after)
        if w == WINDOWS - 1:
            scratch.append(pltpu.VMEM(acc_shape, F))
        if w >= 4:
            data += halos
            scratch += [pltpu.VMEM((24, QUART, 32), B), pltpu.VMEM((24, 16, QUART), B)]
        outs = [(2, LEAVES * PTS)] * 4 if w == WINDOWS - 1 else [acc_shape]
        data += carried
        result = call(
            functools.partial(near_kernel, w, len(carried)),
            [*outs, *extra, *(v.shape for v in carried)],
            [SMEM] + [VMEM] * (len(data) - 1),
            scratch,
            micros=9,
        )(*data)
        if w == WINDOWS - 1:
            whole = result
            break
        acc = result[0]
        if w == 0:
            cw, to_before, to_after = result[1:4]
            up = lax.ppermute(to_before, "leaf", [(i + 1, i) for i in range(count - 1)])
        if w == 1:
            down = lax.ppermute(result[2], "leaf", [(i, i + 1) for i in range(count - 1)])
            halos = [down, up]
        after = jnp.concatenate([result[1 + len(extra)], swapped], 0)
    other = swapped

    level = jnp.asarray([k for k in range(5) for _ in range(64 >> k)], jnp.int32)[None, :]
    owner = lax.shift_right_logical(far_pairs, 4 - level)
    inside = far_pairs & (lax.shift_left(jnp.int32(1), 4 - level) - 1)
    start = jnp.asarray([LEVEL_ROW[k] for k in range(5) for _ in range(64 >> k)], jnp.int32)[None, :]
    apart = device ^ owner
    rows = ((apart & 1) * (count // 2) + (apart >> 1)) * 32 + start + inside
    back = [swap_rhs(whole[2], 2)]
    coupling = coupling.transpose(0, 2, 3, 1)
    scratch = [pltpu.VMEM((128, 2 * RANK), F), pltpu.VMEM((2, RANK, PAIRS), F)]
    table, upper, passed = call(
        first_kernel,
        [(2048, 2 * RANK), (2, 16, RANK), (2, LEAVES * PTS)],
        [SMEM] + [VMEM] * 4,
        scratch,
        micros=0.5,
    )(rows, after, other, coupling, whole[1])
    back.append(swap_rhs(passed, 1))
    coefficients, passed = call(
        second_kernel,
        [(LEAVES, 8, RANK), (2, LEAVES * PTS)],
        [SMEM] + [VMEM] * 5,
        [*scratch, pltpu.VMEM((32, 8, RANK), F)],
        micros=0.5,
    )(rows, table, coupling, upper, transfer, whole[3])
    back.append(swap_rhs(passed, 3))
    (distant,) = call(
        expand_kernel, [(2, LEAVES * PTS)], [VMEM] * 2 + [ANY], micros=0.3
    )(coefficients, leaf_basis, passed)
    return distant + whole[0] + back[0] + back[1] + back[2]


def solution(mesh):
    return jax.shard_map(
        shards,
        mesh=mesh,
        in_specs=(
            P(None, "leaf"),
            P("rhs", "leaf"),
            P("leaf", None, None),
            P("leaf", None, None, None),
            P("leaf", None, None, None),
            P("leaf", None),
            P("leaf", None),
            P("leaf"),
        ),
        out_specs=P("rhs", "leaf"),
        check_vma=False,
    )
```

```python
import functools

import jax
import jax.numpy as jnp
from jax import lax
from jax.experimental import pallas as pl
from jax.experimental.pallas import tpu as pltpu
from jax.sharding import PartitionSpec as P

F = jnp.float32
B = jnp.bfloat16
NN = (((1,), (0,)), ((), ()))
NT = (((1,), (1,)), ((), ()))
HI = lax.Precision.HIGHEST

FAR = 8
STRIP = 4
LEAVES = 16
PTS = 1024
QUART = 256
RANK = 64
NEAR = 9
RHS = 4
NX, NZ, NC = 4, 8, 2
LEVEL_ROW = (0, 16, 24, 28, 30)
TRANSFER_OFFSETS = (0, 8, 12, 14)
RATE = -4.0 * 1.4426950408889634
S_LIMB = (0, 0, 1, 1, 0, 2, 1, 2)
T_LIMB = (0, 1, 0, 1, 2, 0, 2, 1)
PAIRS = 124
WINDOWS = 6
SINGLE = 80
ANY = pl.BlockSpec(memory_space=pl.ANY)
HBM = pl.BlockSpec(memory_space=pltpu.HBM)
VMEM = pl.BlockSpec(memory_space=pltpu.VMEM)
SMEM = pl.BlockSpec(memory_space=pltpu.SMEM)
PARAMS = pltpu.CompilerParams(vmem_limit_bytes=48 * 2**20)


def dot(a, b, dims):
    return lax.dot_general(a, b, dims, preferred_element_type=F)


def dot_hi(a, b, dims):
    return lax.dot_general(a, b, dims, preferred_element_type=F, precision=HI)


def call(kernel, outs, in_specs, scratch=(), micros=1.0, smem_outs=0):
    outs = [v if isinstance(v, jax.ShapeDtypeStruct) else jax.ShapeDtypeStruct(v, F) for v in outs]
    return pl.pallas_call(
        kernel,
        out_shape=outs,
        in_specs=in_specs,
        out_specs=[SMEM if n < smem_outs else VMEM for n in range(len(outs))],
        scratch_shapes=list(scratch),
        compiler_params=PARAMS,
        cost_estimate=pl.CostEstimate(
            flops=int(micros * 10**9), bytes_accessed=10**5, transcendentals=0
        ),
    )


def limbs(v):
    first = v.astype(B).astype(F)
    rest = v - first
    second = rest.astype(B).astype(F)
    return first, second, rest - second


def pick(row, values, rest):
    out = rest
    for n, v in reversed(list(enumerate(values))):
        out = jnp.where(row == n, v, out)
    return out


def source_rows(x, y):
    shape = (8, x.shape[1])
    row = lax.broadcasted_iota(jnp.int32, shape, 0)
    x, y = jnp.broadcast_to(x, shape), jnp.broadcast_to(y, shape)
    lx, ly, ls = limbs(-2.0 * x), limbs(-2.0 * y), limbs(x * x + y * y)
    zero = jnp.zeros(shape, F)
    one = zero + 1.0
    return jnp.concatenate(
        [
            pick(row, [lx[a] for a in S_LIMB], zero),
            pick(row, [ly[a] for a in S_LIMB], zero),
            pick(row, [one, one, one, *ls], zero),
            pick(row, [*lx, *ly], zero),
        ],
        axis=0,
    )


def target_rows(x, y):
    shape = (8, x.shape[1])
    row = lax.broadcasted_iota(jnp.int32, shape, 0)
    lx, ly = (limbs(jnp.broadcast_to(v, shape)) for v in (x, y))
    zero = jnp.zeros(shape, F)
    return jnp.concatenate(
        [pick(row, [lx[b] for b in T_LIMB], zero), pick(row, [ly[b] for b in T_LIMB], zero)], axis=0
    ).astype(B)


def prep_kernel(meta, list_hbm, count_hbm, coords, lists, sf, tab, place, near_list, near_count, sems):
    copies = [
        pltpu.make_async_copy(list_hbm, near_list, sems.at[0]),
        pltpu.make_async_copy(count_hbm, near_count, sems.at[1]),
    ]
    for copy in copies:
        copy.start()
    first, r = meta[0], meta[1]
    for i in range(LEAVES):
        source = pl.ds(pl.multiple_of(r * QUART + i * PTS, QUART), QUART)
        place[:, i * QUART : (i + 1) * QUART] = coords[:, source]
    for n in range(4):
        xy = place[:, 4 * n * QUART : 4 * (n + 1) * QUART] - 0.5
        put_sources(xy, sf, 4 * n)
    for i in range(LEAVES):
        xy = coords[:, i * PTS : (i + 1) * PTS] - 0.5
        tab[i] = target_rows(xy[0:1], xy[1:2])
    for copy in copies:
        copy.wait()

    def put(p, *values):
        for field, value in zip((0, 1, 2, 3, 4, 6), values):
            lists[field, p] = value

    def leaf_pairs(i, counts):
        def slot(s, counts):
            local = near_list[i, s] - first
            before, after = local < 0, local >= LEAVES
            over = (before | after).astype(jnp.int32)
            both = 1 - over
            same = (local == i).astype(jnp.int32)
            later = (local > i).astype(jnp.int32) * both
            p = jnp.where(over == 1, SINGLE + LEAVES + counts[1], counts[0])
            p = jnp.where(same == 1, SINGLE + i, p)

            @pl.when(over + same + later > 0)
            def _():
                put(
                    p,
                    i,
                    jnp.where(before, local + 20, jnp.where(after, local + 4, local)),
                    i,
                    lax.shift_right_arithmetic(local, 2) - lax.shift_right_arithmetic(i, 2),
                    (local & 3) - (i & 3),
                    local,
                )

            return counts[0] + later, counts[1] + over

        return lax.fori_loop(0, near_count[i], slot, counts)

    twice, over = lax.fori_loop(0, LEAVES, leaf_pairs, (jnp.int32(0), jnp.int32(0)))
    put(twice, 0, 0, LEAVES, 0, 0, LEAVES)
    for p in range(4):
        put(SINGLE + LEAVES + over + p, 0, 0, LEAVES, 0, 0, LEAVES)
    lists[5, 0] = (twice + 1) & -2
    lists[5, 1] = LEAVES + over
    lists[5, 2] = r


def put_sources(xy, sf, at):
    rows = source_rows(xy[0:1], xy[1:2])
    rows = jnp.concatenate([rows[:, n * QUART : (n + 1) * QUART] for n in range(4)], axis=0)
    turned = rows.T
    for n in range(4):
        sf[at + n] = turned[:, n * 32 : (n + 1) * 32].astype(B)


def weights(c):
    high = c.astype(B).astype(F)
    return jnp.concatenate([high, c - high], axis=0).astype(B)


def near_kernel(w, n_carried, *refs):
    refs = list(refs)

    def take(n):
        taken = refs[:n]
        del refs[:n]
        return taken

    last = w == WINDOWS - 1
    lists, coords, tab, sf = take(4)
    if w == 0:
        own, first, second, place = take(4)
    else:
        cw, call_w, acc_in, quart_in = take(4)
    if w >= WINDOWS - 2:
        halos = take(2)
    carried = take(n_carried)
    outs = take(4 if last else 2)
    if w == 0:
        cw, call_w, to_before, to_after = take(4)
    for ref, out in zip(carried, take(n_carried)):
        out[...] = ref[...]
    kh_a, kl_a, kh_b, kl_b = take(4)
    acc, quart = take(2) if last else outs
    r = lists[5, 2]
    mine = pl.ds(pl.multiple_of(r * QUART, QUART), QUART)

    if w == 0:
        for j in range(LEAVES):
            at = slice(j * PTS, (j + 1) * PTS)
            call_w[j] = weights(jnp.concatenate([own[:, at], first[:, at], second[:, at]], axis=0))
            cw[j] = call_w[j, :, mine]
        for ref, start in ((to_before, 0), (to_after, 12)):
            ref[0:2] = place[:, start * QUART : (start + 4) * QUART]
            for j in range(4):
                at = slice(j * QUART, (j + 1) * QUART)
                source = pl.ds(pl.multiple_of(r * QUART + (start + j) * PTS, QUART), QUART)
                ref[2:4, at] = own[:, source]
                ref[4:6, at] = first[:, source]
                ref[6:10, at] = second[:, source]
        acc[...] = jnp.zeros_like(acc)
        quart[...] = jnp.zeros_like(quart)
    else:
        acc[...] = acc_in[...]
        quart[...] = quart_in[...]
    if w >= WINDOWS - 2:
        sf_own, cw_own = sf, cw
        sf, cw = take(2)
        sf[0:LEAVES] = sf_own[...]
        cw[0:LEAVES] = cw_own[...]
        for n, halo in enumerate(halos):
            put_sources(halo[0:2] - 0.5, sf, LEAVES + 4 * n)
            for j in range(4):
                cw[LEAVES + 4 * n + j] = weights(halo[2:10, j * QUART : (j + 1) * QUART])

    n_twice, n_single = lists[5, 0], lists[5, 1]

    def bounds(n):
        if n == 0:
            return jnp.int32(0), jnp.int32(0)
        if n == WINDOWS:
            return n_twice, n_single
        at = lax.div((3 * n_twice + 2 * n_single) * n, WINDOWS)
        here = n_single if n > WINDOWS - 2 else LEAVES
        single = jnp.maximum(lax.shift_right_arithmetic(at - 3 * n_twice, 1), 0)
        return jnp.minimum(n_twice, lax.div(at, 3)) & -2, jnp.minimum(here, single) & -2

    (twice_0, single_0), (twice_1, single_1) = bounds(w), bounds(w + 1)

    row = lax.broadcasted_iota(jnp.int32, (8, PTS), 0)
    low, middle = row < 3, (row >= 3) & (row < 6)
    ones = jnp.where(middle, 1.0, 0.0)

    def evaluate(p, kh, kl):
        i, j = lists[0, p], lists[1, p]
        ox, oy = lists[3, p].astype(F), lists[4, p].astype(F)
        xy = coords[:, pl.ds(pl.multiple_of(i * PTS, PTS), PTS)] - 0.5
        x = jnp.broadcast_to(xy[0:1], (8, PTS)) - ox
        y = jnp.broadcast_to(xy[1:2], (8, PTS)) - oy
        ls = limbs(x * x + y * y)
        squares = pick(row, ls, ones)
        offsets = jnp.where(low, -ox, jnp.where(middle, -oy, 0.0))
        t_rows = jnp.concatenate(
            [tab[i], jnp.concatenate([squares, offsets], axis=0).astype(B)], axis=0
        )
        s_rows = sf[j]
        for c in range(4):
            lanes = slice(c * 256, (c + 1) * 256)
            dist2 = dot(s_rows, t_rows[:, lanes], NN)
            for g in range(16):
                at = slice(g * 16, (g + 1) * 16)
                d2 = jnp.maximum(dist2[at], 1e-35)
                k = jnp.exp2((d2 * lax.rsqrt(d2)) * RATE)
                high = k.astype(B)
                kh[at, lanes] = high
                kl[at, lanes] = (k - high.astype(F)).astype(B)

    def multiply(p, kh, kl, both):
        i, j = lists[0, p], lists[1, p]
        high, low_part = kh[...], kl[...]
        acc[lists[2, p]] += dot(cw[j], high, NN) + dot(cw[j], low_part, NN)
        if both:
            quart[lists[6, p]] += dot(call_w[i], high, NT) + dot(call_w[i], low_part, NT)

    def run(begin, end, both):
        def step(n, _):
            p = begin + 2 * n
            evaluate(p, kh_a, kl_a)
            multiply(jnp.maximum(p - 1, begin), kh_b, kl_b, both)
            evaluate(p + 1, kh_b, kl_b)
            multiply(p, kh_a, kl_a, both)
            return 0

        steps = (end - begin + 1) // 2

        @pl.when(steps > 0)
        def _():
            kh_b[...] = jnp.zeros_like(kh_b)
            kl_b[...] = jnp.zeros_like(kl_b)
            lax.fori_loop(0, steps, step, 0)
            multiply(begin + 2 * steps - 1, kh_b, kl_b, both)

    run(twice_0, twice_1, True)
    run(single_0 + SINGLE, single_1 + SINGLE, False)

    if last:
        for i in range(LEAVES):
            v = (acc[i, 0:8, :] + acc[i, 8:16, :]) * (PTS**-0.5)
            for k in range(RHS):
                outs[k][:, i * PTS : (i + 1) * PTS] = v[2 * k : 2 * k + 2]
            q = (quart[i, 0:8, :] + quart[i, 8:16, :]) * (PTS**-0.5)
            at = pl.ds(pl.multiple_of(r * QUART + i * PTS, QUART), QUART)
            for k in range(RHS):
                outs[k][:, at] += q[2 * k : 2 * k + 2]


def bf16(*shape):
    return jax.ShapeDtypeStruct(shape, B)


def split_rows(v):
    high = v.astype(B).astype(F)
    return jnp.concatenate([high, v - high], axis=0).astype(B)


def split_dot(rows, matrix, dims):
    high = matrix.astype(B)
    low = (matrix - high.astype(F)).astype(B)
    v = dot(rows, high, dims) + dot(rows, low, dims)
    return v[0:8] + v[8:16]


def up_kernel(charges, basis, transfer, _, out):
    row = lax.broadcasted_iota(jnp.int32, (8, PTS), 0)

    def put(at, v):
        out[at : at + 1, 0:RANK] = v[0:1]
        out[at : at + 1, RANK : 2 * RANK] = v[1:2]

    current = []
    for i in range(LEAVES):
        c = charges[:, i * PTS : (i + 1) * PTS]
        c = jnp.where(row == 0, c[0:1], jnp.where(row == 1, c[1:2], 0.0))
        v = split_dot(split_rows(c), basis[i], NT)
        put(i, v)
        current.append(v)
    for level in range(1, 5):
        per_block = 8 >> (level - 1)
        lifted = [
            dot_hi(v, transfer[d // per_block, TRANSFER_OFFSETS[level - 1] + d % per_block], NN)
            for d, v in enumerate(current)
        ]
        current = [lifted[d] + lifted[d + 1] for d in range(0, len(lifted), 2)]
        for d, v in enumerate(current):
            put(LEVEL_ROW[level] + d, v)
    out[31:32, :] = jnp.zeros((1, 2 * RANK), F)


def couple(block, rows, table, coupling, picked, products):
    picked[120:128, :] = jnp.zeros((8, 2 * RANK), F)
    for q in range(PAIRS):
        picked[q : q + 1, :] = table[pl.ds(rows[block, q], 1), :]
    turned = picked[...].T
    g = [turned[c * RANK : (c + 1) * RANK, 0:PAIRS] for c in range(2)]

    def part(n, _):
        at = pl.ds(pl.multiple_of(n * 8, 8), 8)
        b = coupling[block, at]
        for c in range(2):
            products[c, at, :] = jnp.sum(b * g[c][None], axis=1)
        return 0

    lax.fori_loop(0, RANK // 8, part, 0)
    pair = lax.broadcasted_iota(jnp.int32, (16, PAIRS), 1)
    target = lax.broadcasted_iota(jnp.int32, (16, PAIRS), 0)
    member = jnp.where(lax.shift_right_arithmetic(pair, 3) == target, 1.0, 0.0)
    return [dot_hi(member, products[c], NT) for c in range(2)]


def down_kernel(rows, own, other, coupling, transfer, basis, out, table, picked, products, held):
    half = own.shape[0]
    table[0:half, :] = own[...]
    table[half : 2 * half, :] = other[...]
    held[...] = jnp.zeros_like(held)
    for block in range(2):
        for c, t in enumerate(couple(block, rows, table, coupling, picked.at[block], products.at[block])):
            for n in range(16):
                held[16 * block + n, c : c + 1, :] = t[n : n + 1]
    current = [held[15] + held[31]]
    first = (0, 8, 12, 14)
    for level in range(4, 0, -1):
        per_block = 8 >> (level - 1)
        current = [
            held[16 * (d // per_block) + first[level - 1] + d % per_block]
            + dot_hi(
                current[d // 2],
                transfer[d // per_block, TRANSFER_OFFSETS[level - 1] + d % per_block],
                NT,
            )
            for d in range(2 * per_block)
        ]
    for i in range(LEAVES):
        v = split_dot(split_rows(current[i]), basis[i], NN)
        out[:, i * PTS : (i + 1) * PTS] = v[0:2]


def shards(coords, charges, leaf_basis, transfer, coupling, far_pairs, near_list, near_count):
    device = lax.axis_index("leaf").astype(jnp.int32)
    rhs_index = lax.axis_index("rhs").astype(jnp.int32)
    meta = jnp.stack([device * LEAVES, rhs_index])
    count = NX * NZ * NC

    def swap_rhs(v, k):
        return lax.ppermute(v, "rhs", [(i, i ^ k) for i in range(RHS)])

    def swap_leaf(v, bit):
        return lax.ppermute(v, "leaf", [(d, d ^ bit) for d in range(count)])

    first = swap_rhs(charges, 1)
    lists, sf, tab, place = call(
        prep_kernel,
        [
            jax.ShapeDtypeStruct((8, 320), jnp.int32),
            bf16(LEAVES, QUART, 32),
            bf16(LEAVES, 16, PTS),
            (2, LEAVES * QUART),
        ],
        [SMEM, HBM, HBM, VMEM],
        [
            pltpu.SMEM((LEAVES, NEAR), jnp.int32),
            pltpu.SMEM((LEAVES,), jnp.int32),
            pltpu.SemaphoreType.DMA((2,)),
        ],
        micros=4,
        smem_outs=1,
    )(meta, near_list, near_count, coords)
    onward = jnp.concatenate([charges, first], 0)
    second = swap_rhs(onward, 2)
    (table,) = call(up_kernel, [(32, 2 * RANK)], [VMEM] * 3 + [ANY], micros=4)(
        charges, leaf_basis, transfer, onward
    )

    acc_shape, quart_shape = (LEAVES + 1, 16, PTS), (LEAVES + 1, 16, QUART)
    halo_shape = (10, 4 * QUART)
    values = [pltpu.VMEM((QUART, PTS), B)] * 4
    after, halos = table, []
    for w, bit in enumerate((2, 4, 8, 16, 32, 1)):
        swapped = swap_leaf(after, bit)
        data, extra, scratch = [lists, coords, tab, sf], [], [*values]
        if w == 0:
            data += [charges, first, second, place]
            extra = [bf16(LEAVES, 16, QUART), bf16(LEAVES, 16, PTS), halo_shape, halo_shape]
        else:
            data += [cw, call_w, acc, quart]
        if w == WINDOWS - 1:
            scratch += [pltpu.VMEM(acc_shape, F), pltpu.VMEM(quart_shape, F)]
        if w >= WINDOWS - 2:
            data += halos
            scratch += [pltpu.VMEM((24, QUART, 32), B), pltpu.VMEM((24, 16, QUART), B)]
        carried = [after] if w < WINDOWS - 1 else []
        outs = [(2, LEAVES * PTS)] * 4 if w == WINDOWS - 1 else [acc_shape, quart_shape]
        result = call(
            functools.partial(near_kernel, w, len(carried)),
            [*outs, *extra, *(v.shape for v in carried)],
            [SMEM] + [VMEM] * (len(data) + len(carried) - 1),
            scratch,
            micros=9,
        )(*data, *carried)
        if w == WINDOWS - 1:
            whole = result
            break
        acc, quart = result[:2]
        after = jnp.concatenate([result[-1], swapped], 0)
        if w == 0:
            cw, call_w, to_before, to_after = result[2:6]
            up = lax.ppermute(to_before, "leaf", [(i + 1, i) for i in range(count - 1)])
            down = lax.ppermute(to_after, "leaf", [(i, i + 1) for i in range(count - 1)])
            halos = [down, up]
    other = swapped

    level = jnp.asarray([k for k in range(5) for _ in range(64 >> k)], jnp.int32)[None, :]
    owner = lax.shift_right_logical(far_pairs, 4 - level)
    inside = far_pairs & (lax.shift_left(jnp.int32(1), 4 - level) - 1)
    start = jnp.asarray([LEVEL_ROW[k] for k in range(5) for _ in range(64 >> k)], jnp.int32)[None, :]
    apart = device ^ owner
    rows = ((apart & 1) * (count // 2) + (apart >> 1)) * 32 + start + inside
    back = [swap_rhs(whole[k], k) for k in (2, 1, 3)]
    (distant,) = call(
        down_kernel,
        [(2, LEAVES * PTS)],
        [SMEM] + [VMEM] * 5,
        [
            pltpu.VMEM((2048, 2 * RANK), F),
            pltpu.VMEM((2, 128, 2 * RANK), F),
            pltpu.VMEM((2, 2, RANK, PAIRS), F),
            pltpu.VMEM((32, 8, RANK), F),
        ],
        micros=8,
    )(rows, after, other, coupling.transpose(0, 2, 3, 1), transfer, leaf_basis)
    return distant + whole[0] + back[0] + back[1] + back[2]


def solution(mesh):
    return jax.shard_map(
        shards,
        mesh=mesh,
        in_specs=(
            P(None, "leaf"),
            P("rhs", "leaf"),
            P("leaf", None, None),
            P("leaf", None, None, None),
            P("leaf", None, None, None),
            P("leaf", None),
            P("leaf", None),
            P("leaf"),
        ),
        out_specs=P("rhs", "leaf"),
        check_vma=False,
    )
```

```python
import functools

import jax
import jax.numpy as jnp
from jax import lax
from jax.experimental import pallas as pl
from jax.experimental.pallas import tpu as pltpu
from jax.sharding import PartitionSpec as P

F = jnp.float32
B = jnp.bfloat16
NN = (((1,), (0,)), ((), ()))
NT = (((1,), (1,)), ((), ()))
HI = lax.Precision.HIGHEST

FAR = 8
STRIP = 4
LEAVES = 16
PTS = 1024
QUART = 256
RANK = 64
NEAR = 9
RHS = 4
NX, NZ, NC = 4, 8, 2
LEVEL_ROW = (0, 16, 24, 28, 30)
TRANSFER_OFFSETS = (0, 8, 12, 14)
RATE = -4.0 * 1.4426950408889634
S_LIMB = (0, 0, 1, 1, 0, 2, 1, 2)
T_LIMB = (0, 1, 0, 1, 2, 0, 2, 1)
PAIRS = 124
WINDOWS = 6
SINGLE = 80
ANY = pl.BlockSpec(memory_space=pl.ANY)
HBM = pl.BlockSpec(memory_space=pltpu.HBM)
VMEM = pl.BlockSpec(memory_space=pltpu.VMEM)
SMEM = pl.BlockSpec(memory_space=pltpu.SMEM)
PARAMS = pltpu.CompilerParams(vmem_limit_bytes=24 * 2**20)


def dot(a, b, dims):
    return lax.dot_general(a, b, dims, preferred_element_type=F)


def dot_hi(a, b, dims):
    return lax.dot_general(a, b, dims, preferred_element_type=F, precision=HI)


def call(kernel, outs, in_specs, scratch=(), micros=1.0, smem_outs=0):
    outs = [v if isinstance(v, jax.ShapeDtypeStruct) else jax.ShapeDtypeStruct(v, F) for v in outs]
    return pl.pallas_call(
        kernel,
        out_shape=outs,
        in_specs=in_specs,
        out_specs=[SMEM if n < smem_outs else VMEM for n in range(len(outs))],
        scratch_shapes=list(scratch),
        compiler_params=PARAMS,
        cost_estimate=pl.CostEstimate(
            flops=int(micros * 10**9), bytes_accessed=10**5, transcendentals=0
        ),
    )


def limbs(v):
    first = v.astype(B).astype(F)
    rest = v - first
    second = rest.astype(B).astype(F)
    return first, second, rest - second


def pick(row, values, rest):
    out = rest
    for n, v in reversed(list(enumerate(values))):
        out = jnp.where(row == n, v, out)
    return out


def source_rows(x, y):
    shape = (8, x.shape[1])
    row = lax.broadcasted_iota(jnp.int32, shape, 0)
    x, y = jnp.broadcast_to(x, shape), jnp.broadcast_to(y, shape)
    lx, ly, ls = limbs(-2.0 * x), limbs(-2.0 * y), limbs(x * x + y * y)
    zero = jnp.zeros(shape, F)
    one = zero + 1.0
    return jnp.concatenate(
        [
            pick(row, [lx[a] for a in S_LIMB], zero),
            pick(row, [ly[a] for a in S_LIMB], zero),
            pick(row, [one, one, one, *ls], zero),
            pick(row, [*lx, *ly], zero),
        ],
        axis=0,
    )


def target_rows(x, y):
    shape = (8, x.shape[1])
    row = lax.broadcasted_iota(jnp.int32, shape, 0)
    lx, ly = (limbs(jnp.broadcast_to(v, shape)) for v in (x, y))
    zero = jnp.zeros(shape, F)
    return jnp.concatenate(
        [pick(row, [lx[b] for b in T_LIMB], zero), pick(row, [ly[b] for b in T_LIMB], zero)], axis=0
    ).astype(B)


def prep_kernel(meta, list_hbm, count_hbm, coords, _, lists, sf, tab, place, near_list, near_count, sems):
    copies = [
        pltpu.make_async_copy(list_hbm, near_list, sems.at[0]),
        pltpu.make_async_copy(count_hbm, near_count, sems.at[1]),
    ]
    for copy in copies:
        copy.start()
    first, r = meta[0], meta[1]
    for i in range(LEAVES):
        source = pl.ds(pl.multiple_of(r * QUART + i * PTS, QUART), QUART)
        place[:, i * QUART : (i + 1) * QUART] = coords[:, source]
    for n in range(4):
        xy = place[:, 4 * n * QUART : 4 * (n + 1) * QUART] - 0.5
        put_sources(xy, sf, 4 * n)
    for i in range(LEAVES):
        xy = coords[:, i * PTS : (i + 1) * PTS] - 0.5
        tab[i] = target_rows(xy[0:1], xy[1:2])
    for copy in copies:
        copy.wait()

    def put(p, *values):
        for field, value in zip((0, 1, 2, 3, 4, 6), values):
            lists[field, p] = value

    def leaf_pairs(i, counts):
        def slot(s, counts):
            local = near_list[i, s] - first
            before, after = local < 0, local >= LEAVES
            over = (before | after).astype(jnp.int32)
            both = 1 - over
            same = (local == i).astype(jnp.int32)
            later = (local > i).astype(jnp.int32) * both
            p = jnp.where(over == 1, SINGLE + LEAVES + counts[1], counts[0])
            p = jnp.where(same == 1, SINGLE + i, p)

            @pl.when(over + same + later > 0)
            def _():
                put(
                    p,
                    i,
                    jnp.where(before, local + 20, jnp.where(after, local + 4, local)),
                    i,
                    lax.shift_right_arithmetic(local, 2) - lax.shift_right_arithmetic(i, 2),
                    (local & 3) - (i & 3),
                    local,
                )

            return counts[0] + later, counts[1] + over

        return lax.fori_loop(0, near_count[i], slot, counts)

    twice, over = lax.fori_loop(0, LEAVES, leaf_pairs, (jnp.int32(0), jnp.int32(0)))
    put(twice, 0, 0, LEAVES, 0, 0, LEAVES)
    for p in range(4):
        put(SINGLE + LEAVES + over + p, 0, 0, LEAVES, 0, 0, LEAVES)
    lists[5, 0] = (twice + 1) & -2
    lists[5, 1] = LEAVES + over
    lists[5, 2] = r


def put_sources(xy, sf, at):
    rows = source_rows(xy[0:1], xy[1:2])
    rows = jnp.concatenate([rows[:, n * QUART : (n + 1) * QUART] for n in range(4)], axis=0)
    turned = rows.T
    for n in range(4):
        sf[at + n] = turned[:, n * 32 : (n + 1) * 32].astype(B)


def weights(c):
    high = c.astype(B).astype(F)
    return jnp.concatenate([high, c - high], axis=0).astype(B)


def near_kernel(w, n_carried, *refs):
    refs = list(refs)

    def take(n):
        taken = refs[:n]
        del refs[:n]
        return taken

    last = w == WINDOWS - 1
    lists, coords, tab, sf = take(4)
    if w == 0:
        own, first, second, place = take(4)
    else:
        cw, call_w, acc_in, quart_in = take(4)
    if w == WINDOWS - 2:
        halos = take(2)
    carried = take(n_carried)
    outs = take(4 if last else 2)
    if w == 0:
        cw, call_w, to_before, to_after = take(4)
    if w == WINDOWS - 2:
        sf_own, cw_own = sf, cw
        sf, cw = take(2)
    for ref, out in zip(carried, take(n_carried)):
        out[...] = ref[...]
    kh_a, kl_a, kh_b, kl_b = take(4)
    acc, quart = take(2) if last else outs
    r = lists[5, 2]
    mine = pl.ds(pl.multiple_of(r * QUART, QUART), QUART)

    if w == 0:
        for j in range(LEAVES):
            at = slice(j * PTS, (j + 1) * PTS)
            call_w[j] = weights(jnp.concatenate([own[:, at], first[:, at], second[:, at]], axis=0))
            cw[j] = call_w[j, :, mine]
        for ref, start in ((to_before, 0), (to_after, 12)):
            ref[0:2] = place[:, start * QUART : (start + 4) * QUART]
            for j in range(4):
                at = slice(j * QUART, (j + 1) * QUART)
                source = pl.ds(pl.multiple_of(r * QUART + (start + j) * PTS, QUART), QUART)
                ref[2:4, at] = own[:, source]
                ref[4:6, at] = first[:, source]
                ref[6:10, at] = second[:, source]
        acc[...] = jnp.zeros_like(acc)
        quart[...] = jnp.zeros_like(quart)
    else:
        acc[...] = acc_in[...]
        quart[...] = quart_in[...]
    if w == WINDOWS - 2:
        sf[0:LEAVES] = sf_own[...]
        cw[0:LEAVES] = cw_own[...]
        for n, halo in enumerate(halos):
            put_sources(halo[0:2] - 0.5, sf, LEAVES + 4 * n)
            for j in range(4):
                cw[LEAVES + 4 * n + j] = weights(halo[2:10, j * QUART : (j + 1) * QUART])

    n_twice, n_single = lists[5, 0], lists[5, 1]

    def bounds(n):
        if n == 0:
            return jnp.int32(0), jnp.int32(0)
        if n == WINDOWS:
            return n_twice, n_single
        at = lax.div((3 * n_twice + 2 * n_single) * n, WINDOWS)
        here = n_single if n > WINDOWS - 2 else LEAVES
        single = jnp.maximum(lax.shift_right_arithmetic(at - 3 * n_twice, 1), 0)
        return jnp.minimum(n_twice, lax.div(at, 3)) & -2, jnp.minimum(here, single) & -2

    (twice_0, single_0), (twice_1, single_1) = bounds(w), bounds(w + 1)

    row = lax.broadcasted_iota(jnp.int32, (8, PTS), 0)
    low, middle = row < 3, (row >= 3) & (row < 6)
    ones = jnp.where(middle, 1.0, 0.0)

    def evaluate(p, kh, kl):
        i, j = lists[0, p], lists[1, p]
        ox, oy = lists[3, p].astype(F), lists[4, p].astype(F)
        xy = coords[:, pl.ds(pl.multiple_of(i * PTS, PTS), PTS)] - 0.5
        x = jnp.broadcast_to(xy[0:1], (8, PTS)) - ox
        y = jnp.broadcast_to(xy[1:2], (8, PTS)) - oy
        ls = limbs(x * x + y * y)
        squares = pick(row, ls, ones)
        offsets = jnp.where(low, -ox, jnp.where(middle, -oy, 0.0))
        t_rows = jnp.concatenate(
            [tab[i], jnp.concatenate([squares, offsets], axis=0).astype(B)], axis=0
        )
        s_rows = sf[j]
        for c in range(4):
            lanes = slice(c * 256, (c + 1) * 256)
            dist2 = dot(s_rows, t_rows[:, lanes], NN)
            for g in range(16):
                at = slice(g * 16, (g + 1) * 16)
                d2 = jnp.maximum(dist2[at], 1e-35)
                k = jnp.exp2((d2 * lax.rsqrt(d2)) * RATE)
                high = k.astype(B)
                kh[at, lanes] = high
                kl[at, lanes] = (k - high.astype(F)).astype(B)

    def multiply(p, kh, kl, both, none=False):
        i, j = lists[0, p], lists[1, p]
        high, low_part = kh[...], kl[...]
        to = jnp.where(none, LEAVES, lists[2, p])
        acc[to] += dot(cw[j], high, NN) + dot(cw[j], low_part, NN)
        if both:
            to = jnp.where(none, LEAVES, lists[6, p])
            quart[to] += dot(call_w[i], high, NT) + dot(call_w[i], low_part, NT)

    def run(begin, end, both):
        def step(n, _):
            p = begin + 2 * n
            evaluate(p, kh_a, kl_a)
            multiply(jnp.maximum(p - 1, begin), kh_b, kl_b, both, n == 0)
            evaluate(p + 1, kh_b, kl_b)
            multiply(p, kh_a, kl_a, both)
            return 0

        steps = (end - begin + 1) // 2

        @pl.when(steps > 0)
        def _():
            lax.fori_loop(0, steps, step, 0)
            multiply(begin + 2 * steps - 1, kh_b, kl_b, both)

    run(twice_0, twice_1, True)
    run(single_0 + SINGLE, single_1 + SINGLE, False)

    if last:
        for i in range(LEAVES):
            v = (acc[i, 0:8, :] + acc[i, 8:16, :]) * (PTS**-0.5)
            for k in range(RHS):
                outs[k][:, i * PTS : (i + 1) * PTS] = v[2 * k : 2 * k + 2]
            q = (quart[i, 0:8, :] + quart[i, 8:16, :]) * (PTS**-0.5)
            at = pl.ds(pl.multiple_of(r * QUART + i * PTS, QUART), QUART)
            for k in range(RHS):
                outs[k][:, at] += q[2 * k : 2 * k + 2]


def bf16(*shape):
    return jax.ShapeDtypeStruct(shape, B)


def split_rows(v):
    high = v.astype(B).astype(F)
    return jnp.concatenate([high, v - high], axis=0).astype(B)


def split_dot(rows, matrix, dims):
    high = matrix.astype(B)
    low = (matrix - high.astype(F)).astype(B)
    v = dot(rows, high, dims) + dot(rows, low, dims)
    return v[0:8] + v[8:16]


def up_kernel(charges, basis, transfer, out):
    row = lax.broadcasted_iota(jnp.int32, (8, PTS), 0)

    def put(at, v):
        out[at : at + 1, 0:RANK] = v[0:1]
        out[at : at + 1, RANK : 2 * RANK] = v[1:2]

    current = []
    for i in range(LEAVES):
        c = charges[:, i * PTS : (i + 1) * PTS]
        c = jnp.where(row == 0, c[0:1], jnp.where(row == 1, c[1:2], 0.0))
        v = split_dot(split_rows(c), basis[i], NT)
        put(i, v)
        current.append(v)
    for level in range(1, 5):
        per_block = 8 >> (level - 1)
        lifted = [
            dot_hi(v, transfer[d // per_block, TRANSFER_OFFSETS[level - 1] + d % per_block], NN)
            for d, v in enumerate(current)
        ]
        current = [lifted[d] + lifted[d + 1] for d in range(0, len(lifted), 2)]
        for d, v in enumerate(current):
            put(LEVEL_ROW[level] + d, v)
    out[31:32, :] = jnp.zeros((1, 2 * RANK), F)


def couple(block, rows, table, coupling, picked, products):
    picked[120:128, :] = jnp.zeros((8, 2 * RANK), F)
    for q in range(PAIRS):
        picked[q : q + 1, :] = table[pl.ds(rows[block, q], 1), :]
    turned = picked[...].T
    g = [turned[c * RANK : (c + 1) * RANK, 0:PAIRS] for c in range(2)]

    def part(n, _):
        at = pl.ds(pl.multiple_of(n * 8, 8), 8)
        b = coupling[block, at]
        for c in range(2):
            products[c, at, :] = jnp.sum(b * g[c][None], axis=1)
        return 0

    lax.fori_loop(0, RANK // 8, part, 0)
    pair = lax.broadcasted_iota(jnp.int32, (16, PAIRS), 1)
    target = lax.broadcasted_iota(jnp.int32, (16, PAIRS), 0)
    member = jnp.where(lax.shift_right_arithmetic(pair, 3) == target, 1.0, 0.0)
    return [dot_hi(member, products[c], NT) for c in range(2)]


def down_kernel(rows, own, other, coupling, transfer, basis, out, table, picked, products, held):
    half = own.shape[0]
    table[0:half, :] = own[...]
    table[half : 2 * half, :] = other[...]
    held[...] = jnp.zeros_like(held)
    for block in range(2):
        for c, t in enumerate(couple(block, rows, table, coupling, picked.at[block], products.at[block])):
            for n in range(16):
                held[16 * block + n, c : c + 1, :] = t[n : n + 1]
    current = [held[15] + held[31]]
    first = (0, 8, 12, 14)
    for level in range(4, 0, -1):
        per_block = 8 >> (level - 1)
        current = [
            held[16 * (d // per_block) + first[level - 1] + d % per_block]
            + dot_hi(
                current[d // 2],
                transfer[d // per_block, TRANSFER_OFFSETS[level - 1] + d % per_block],
                NT,
            )
            for d in range(2 * per_block)
        ]
    for i in range(LEAVES):
        v = split_dot(split_rows(current[i]), basis[i], NN)
        out[:, i * PTS : (i + 1) * PTS] = v[0:2]


def shards(coords, charges, leaf_basis, transfer, coupling, far_pairs, near_list, near_count):
    device = lax.axis_index("leaf").astype(jnp.int32)
    rhs_index = lax.axis_index("rhs").astype(jnp.int32)
    meta = jnp.stack([device * LEAVES, rhs_index])
    count = NX * NZ * NC

    def swap_rhs(v, k):
        return lax.ppermute(v, "rhs", [(i, i ^ k) for i in range(RHS)])

    def swap_leaf(v, bit):
        return lax.ppermute(v, "leaf", [(d, d ^ bit) for d in range(count)])

    first = swap_rhs(charges, 1)
    onward = jnp.concatenate([charges, first], 0)
    lists, sf, tab, place = call(
        prep_kernel,
        [
            jax.ShapeDtypeStruct((8, 128), jnp.int32),
            bf16(LEAVES, QUART, 32),
            bf16(LEAVES, 16, PTS),
            (2, LEAVES * QUART),
        ],
        [SMEM, HBM, HBM, VMEM, ANY],
        [
            pltpu.SMEM((LEAVES, NEAR), jnp.int32),
            pltpu.SMEM((LEAVES,), jnp.int32),
            pltpu.SemaphoreType.DMA((2,)),
        ],
        micros=4,
        smem_outs=1,
    )(meta, near_list, near_count, coords, onward)
    second = swap_rhs(onward, 2)
    (table,) = call(up_kernel, [(32, 2 * RANK)], [VMEM] * 3, micros=4)(
        charges, leaf_basis, transfer
    )

    acc_shape, quart_shape = (LEAVES + 1, 16, PTS), (LEAVES + 1, 16, QUART)
    halo_shape = (10, 4 * QUART)
    values = [pltpu.VMEM((QUART, PTS), B)] * 4
    after, halos = table, []
    for w, bit in enumerate((2, 4, 8, 16, 32, 1)):
        swapped = swap_leaf(after, bit)
        data, extra, scratch = [lists, coords, tab, sf], [], [*values]
        if w == 0:
            data += [charges, first, second, place]
            extra = [bf16(LEAVES, 16, QUART), bf16(LEAVES, 16, PTS), halo_shape, halo_shape]
        else:
            data += [cw, call_w, acc, quart]
        if w == WINDOWS - 1:
            scratch += [pltpu.VMEM(acc_shape, F), pltpu.VMEM(quart_shape, F)]
        if w == WINDOWS - 2:
            data += halos
            extra = [bf16(24, QUART, 32), bf16(24, 16, QUART)]
        carried = [after] if w < WINDOWS - 1 else []
        outs = [(2, LEAVES * PTS)] * 4 if w == WINDOWS - 1 else [acc_shape, quart_shape]
        result = call(
            functools.partial(near_kernel, w, len(carried)),
            [*outs, *extra, *(v.shape for v in carried)],
            [SMEM] + [VMEM] * (len(data) + len(carried) - 1),
            scratch,
            micros=9,
        )(*data, *carried)
        if w == WINDOWS - 1:
            whole = result
            break
        acc, quart = result[:2]
        after = jnp.concatenate([result[-1], swapped], 0)
        if w == WINDOWS - 2:
            sf, cw = result[2:4]
        if w == 0:
            cw, call_w, to_before, to_after = result[2:6]
            up = lax.ppermute(to_before, "leaf", [(i + 1, i) for i in range(count - 1)])
            down = lax.ppermute(to_after, "leaf", [(i, i + 1) for i in range(count - 1)])
            halos = [down, up]
    other = swapped

    level = jnp.asarray([k for k in range(5) for _ in range(64 >> k)], jnp.int32)[None, :]
    owner = lax.shift_right_logical(far_pairs, 4 - level)
    inside = far_pairs & (lax.shift_left(jnp.int32(1), 4 - level) - 1)
    start = jnp.asarray([LEVEL_ROW[k] for k in range(5) for _ in range(64 >> k)], jnp.int32)[None, :]
    apart = device ^ owner
    rows = ((apart & 1) * (count // 2) + (apart >> 1)) * 32 + start + inside
    back = [swap_rhs(whole[k], k) for k in (2, 1, 3)]
    (distant,) = call(
        down_kernel,
        [(2, LEAVES * PTS)],
        [SMEM] + [VMEM] * 5,
        [
            pltpu.VMEM((2048, 2 * RANK), F),
            pltpu.VMEM((2, 128, 2 * RANK), F),
            pltpu.VMEM((2, 2, RANK, PAIRS), F),
            pltpu.VMEM((32, 8, RANK), F),
        ],
        micros=8,
    )(rows, after, other, coupling.transpose(0, 2, 3, 1), transfer, leaf_basis)
    return distant + whole[0] + back[0] + back[1] + back[2]


def solution(mesh):
    return jax.shard_map(
        shards,
        mesh=mesh,
        in_specs=(
            P(None, "leaf"),
            P("rhs", "leaf"),
            P("leaf", None, None),
            P("leaf", None, None, None),
            P("leaf", None, None, None),
            P("leaf", None),
            P("leaf", None),
            P("leaf"),
        ),
        out_specs=P("rhs", "leaf"),
        check_vma=False,
    )
```

```python
import functools

import jax
import jax.numpy as jnp
from jax import lax
from jax.experimental import pallas as pl
from jax.experimental.pallas import tpu as pltpu
from jax.sharding import PartitionSpec as P

F = jnp.float32
B = jnp.bfloat16
NN = (((1,), (0,)), ((), ()))
NT = (((1,), (1,)), ((), ()))
HI = lax.Precision.HIGHEST

FAR = 8
STRIP = 4
LEAVES = 16
PTS = 1024
QUART = 256
RANK = 64
NEAR = 9
RHS = 4
NX, NZ, NC = 4, 8, 2
LEVEL_ROW = (0, 16, 24, 28, 30)
TRANSFER_OFFSETS = (0, 8, 12, 14)
RATE = -4.0 * 1.4426950408889634
S_LIMB = (0, 0, 1, 1, 0, 2, 1, 2)
T_LIMB = (0, 1, 0, 1, 2, 0, 2, 1)
PAIRS = 124
WINDOWS = 6
SINGLE = 80
EDGE = 128
SHIFTS = (-8, -1, 2, -4, 32, -16)
ANY = pl.BlockSpec(memory_space=pl.ANY)
HBM = pl.BlockSpec(memory_space=pltpu.HBM)
VMEM = pl.BlockSpec(memory_space=pltpu.VMEM)
SMEM = pl.BlockSpec(memory_space=pltpu.SMEM)
PARAMS = pltpu.CompilerParams(vmem_limit_bytes=24 * 2**20)


def dot(a, b, dims):
    return lax.dot_general(a, b, dims, preferred_element_type=F)


def dot_hi(a, b, dims):
    return lax.dot_general(a, b, dims, preferred_element_type=F, precision=HI)


def call(kernel, outs, in_specs, scratch=(), micros=1.0, smem_outs=0):
    outs = [v if isinstance(v, jax.ShapeDtypeStruct) else jax.ShapeDtypeStruct(v, F) for v in outs]
    return pl.pallas_call(
        kernel,
        out_shape=outs,
        in_specs=in_specs,
        out_specs=[SMEM if n < smem_outs else VMEM for n in range(len(outs))],
        scratch_shapes=list(scratch),
        compiler_params=PARAMS,
        cost_estimate=pl.CostEstimate(
            flops=int(micros * 10**9), bytes_accessed=10**5, transcendentals=0
        ),
    )


def limbs(v):
    first = v.astype(B).astype(F)
    rest = v - first
    second = rest.astype(B).astype(F)
    return first, second, rest - second


def pick(row, values, rest):
    out = rest
    for n, v in reversed(list(enumerate(values))):
        out = jnp.where(row == n, v, out)
    return out


def source_rows(x, y):
    shape = (8, x.shape[1])
    row = lax.broadcasted_iota(jnp.int32, shape, 0)
    x, y = jnp.broadcast_to(x, shape), jnp.broadcast_to(y, shape)
    lx, ly, ls = limbs(-2.0 * x), limbs(-2.0 * y), limbs(x * x + y * y)
    zero = jnp.zeros(shape, F)
    one = zero + 1.0
    return jnp.concatenate(
        [
            pick(row, [lx[a] for a in S_LIMB], zero),
            pick(row, [ly[a] for a in S_LIMB], zero),
            pick(row, [one, one, one, *ls], zero),
            pick(row, [*lx, *ly], zero),
        ],
        axis=0,
    )


def target_rows(x, y):
    shape = (8, x.shape[1])
    row = lax.broadcasted_iota(jnp.int32, shape, 0)
    lx, ly = (limbs(jnp.broadcast_to(v, shape)) for v in (x, y))
    zero = jnp.zeros(shape, F)
    return jnp.concatenate(
        [pick(row, [lx[b] for b in T_LIMB], zero), pick(row, [ly[b] for b in T_LIMB], zero)], axis=0
    ).astype(B)


def prep_kernel(meta, list_hbm, count_hbm, coords, _, lists, sf, tab, place, near_list, near_count, sems):
    copies = [
        pltpu.make_async_copy(list_hbm, near_list, sems.at[0]),
        pltpu.make_async_copy(count_hbm, near_count, sems.at[1]),
    ]
    for copy in copies:
        copy.start()
    first, r = meta[0], meta[1]
    for i in range(LEAVES):
        source = pl.ds(pl.multiple_of(r * QUART + i * PTS, QUART), QUART)
        place[:, i * QUART : (i + 1) * QUART] = coords[:, source]
    for n in range(4):
        xy = place[:, 4 * n * QUART : 4 * (n + 1) * QUART] - 0.5
        put_sources(xy, sf, 4 * n)
    for i in range(LEAVES):
        xy = coords[:, i * PTS : (i + 1) * PTS] - 0.5
        tab[i] = target_rows(xy[0:1], xy[1:2])
    for copy in copies:
        copy.wait()

    def put(p, *values):
        for field, value in zip((0, 1, 2, 3, 4, 6), values):
            lists[field, p] = value

    def leaf_pairs(i, counts):
        def slot(s, counts):
            local = near_list[i, s] - first
            before, after = local < 0, local >= LEAVES
            over = (before | after).astype(jnp.int32)
            both = 1 - over
            same = (local == i).astype(jnp.int32)
            later = (local > i).astype(jnp.int32) * both
            p = jnp.where(over == 1, SINGLE + LEAVES + counts[1], counts[0])
            p = jnp.where(same == 1, SINGLE + i, p)

            @pl.when(over + same + later > 0)
            def _():
                put(
                    p,
                    i,
                    jnp.where(before, local + 20, jnp.where(after, local + 4, local)),
                    i,
                    lax.shift_right_arithmetic(local, 2) - lax.shift_right_arithmetic(i, 2),
                    (local & 3) - (i & 3),
                    local,
                )

            return counts[0] + later, counts[1] + over

        return lax.fori_loop(0, near_count[i], slot, counts)

    twice, over = lax.fori_loop(0, LEAVES, leaf_pairs, (jnp.int32(0), jnp.int32(0)))
    put(twice, 0, 0, LEAVES, 0, 0, LEAVES)
    for p in range(4):
        put(SINGLE + LEAVES + over + p, 0, 0, LEAVES, 0, 0, LEAVES)
    lists[5, 0] = (twice + 1) & -2
    lists[5, 1] = LEAVES + over
    lists[5, 2] = r


def put_sources(xy, sf, at):
    rows = source_rows(xy[0:1], xy[1:2])
    rows = jnp.concatenate([rows[:, n * QUART : (n + 1) * QUART] for n in range(4)], axis=0)
    turned = rows.T
    for n in range(4):
        sf[at + n] = turned[:, n * 32 : (n + 1) * 32].astype(B)


def weights(c):
    high = c.astype(B).astype(F)
    return jnp.concatenate([high, c - high], axis=0).astype(B)


def near_kernel(w, n_carried, *refs):
    refs = list(refs)

    def take(n):
        taken = refs[:n]
        del refs[:n]
        return taken

    last = w == WINDOWS - 1
    lists, coords, tab, sf = take(4)
    if w == 0:
        own, first, second, place = take(4)
    else:
        cw, call_w, acc_in, quart_in = take(4)
    if w == WINDOWS - 2:
        halos = take(2)
    carried = take(n_carried)
    outs = take(4 if last else 2)
    if w == 0:
        cw, call_w, payload = take(3)
    if w == WINDOWS - 2:
        sf_own, cw_own = sf, cw
        sf, cw = take(2)
    for ref, out in zip(carried, take(n_carried)):
        out[...] = ref[...]
    kh_a, kl_a, kh_b, kl_b = take(4)
    acc, quart = take(2) if last else outs
    r = lists[5, 2]
    mine = pl.ds(pl.multiple_of(r * QUART, QUART), QUART)

    if w == 0:
        for j in range(LEAVES):
            at = slice(j * PTS, (j + 1) * PTS)
            call_w[j] = weights(jnp.concatenate([own[:, at], first[:, at], second[:, at]], axis=0))
            cw[j] = call_w[j, :, mine]
        payload[...] = jnp.zeros_like(payload)
        for end, start in enumerate((0, 12)):
            for m in range(8):
                top = end * EDGE + 16 * m
                at = (start + m // 2) * QUART + m % 2 * 128
                payload[top : top + 2] = place[:, at : at + 128]
                at = r * QUART + (start + m // 2) * PTS + m % 2 * 128
                source = pl.ds(pl.multiple_of(at, 128), 128)
                payload[top + 2 : top + 4] = own[:, source]
                payload[top + 4 : top + 6] = first[:, source]
                payload[top + 6 : top + 10] = second[:, source]
        acc[...] = jnp.zeros_like(acc)
        quart[...] = jnp.zeros_like(quart)
    else:
        acc[...] = acc_in[...]
        quart[...] = quart_in[...]
    if w == WINDOWS - 2:
        sf[0:LEAVES] = sf_own[...]
        cw[0:LEAVES] = cw_own[...]
        for n, halo in enumerate(halos):
            halo = jnp.concatenate([halo[16 * m : 16 * m + 10] for m in range(8)], axis=1)
            put_sources(halo[0:2] - 0.5, sf, LEAVES + 4 * n)
            for j in range(4):
                cw[LEAVES + 4 * n + j] = weights(halo[2:10, j * QUART : (j + 1) * QUART])

    n_twice, n_single = lists[5, 0], lists[5, 1]

    def bounds(n):
        if n == 0:
            return jnp.int32(0), jnp.int32(0)
        if n == WINDOWS:
            return n_twice, n_single
        at = lax.div((3 * n_twice + 2 * n_single) * n, WINDOWS)
        here = n_single if n > WINDOWS - 2 else LEAVES
        single = jnp.maximum(lax.shift_right_arithmetic(at - 3 * n_twice, 1), 0)
        return jnp.minimum(n_twice, lax.div(at, 3)) & -2, jnp.minimum(here, single) & -2

    (twice_0, single_0), (twice_1, single_1) = bounds(w), bounds(w + 1)

    row = lax.broadcasted_iota(jnp.int32, (8, PTS), 0)
    low, middle = row < 3, (row >= 3) & (row < 6)
    ones = jnp.where(middle, 1.0, 0.0)

    def evaluate(p, kh, kl):
        i, j = lists[0, p], lists[1, p]
        ox, oy = lists[3, p].astype(F), lists[4, p].astype(F)
        xy = coords[:, pl.ds(pl.multiple_of(i * PTS, PTS), PTS)] - 0.5
        x = jnp.broadcast_to(xy[0:1], (8, PTS)) - ox
        y = jnp.broadcast_to(xy[1:2], (8, PTS)) - oy
        ls = limbs(x * x + y * y)
        squares = pick(row, ls, ones)
        offsets = jnp.where(low, -ox, jnp.where(middle, -oy, 0.0))
        t_rows = jnp.concatenate(
            [tab[i], jnp.concatenate([squares, offsets], axis=0).astype(B)], axis=0
        )
        s_rows = sf[j]
        for c in range(4):
            lanes = slice(c * 256, (c + 1) * 256)
            dist2 = dot(s_rows, t_rows[:, lanes], NN)
            for g in range(16):
                at = slice(g * 16, (g + 1) * 16)
                d2 = jnp.maximum(dist2[at], 1e-35)
                k = jnp.exp2((d2 * lax.rsqrt(d2)) * RATE)
                high = k.astype(B)
                kh[at, lanes] = high
                kl[at, lanes] = (k - high.astype(F)).astype(B)

    def multiply(p, kh, kl, both, none=False):
        i, j = lists[0, p], lists[1, p]
        high, low_part = kh[...], kl[...]
        to = jnp.where(none, LEAVES, lists[2, p])
        acc[to] += dot(cw[j], high, NN) + dot(cw[j], low_part, NN)
        if both:
            to = jnp.where(none, LEAVES, lists[6, p])
            quart[to] += dot(call_w[i], high, NT) + dot(call_w[i], low_part, NT)

    def run(begin, end, both):
        def step(n, _):
            p = begin + 2 * n
            evaluate(p, kh_a, kl_a)
            multiply(jnp.maximum(p - 1, begin), kh_b, kl_b, both, n == 0)
            evaluate(p + 1, kh_b, kl_b)
            multiply(p, kh_a, kl_a, both)
            return 0

        steps = (end - begin + 1) // 2

        @pl.when(steps > 0)
        def _():
            lax.fori_loop(0, steps, step, 0)
            multiply(begin + 2 * steps - 1, kh_b, kl_b, both)

    run(twice_0, twice_1, True)
    run(single_0 + SINGLE, single_1 + SINGLE, False)

    if last:
        for i in range(LEAVES):
            v = (acc[i, 0:8, :] + acc[i, 8:16, :]) * (PTS**-0.5)
            for k in range(RHS):
                outs[k][:, i * PTS : (i + 1) * PTS] = v[2 * k : 2 * k + 2]
            q = (quart[i, 0:8, :] + quart[i, 8:16, :]) * (PTS**-0.5)
            at = pl.ds(pl.multiple_of(r * QUART + i * PTS, QUART), QUART)
            for k in range(RHS):
                outs[k][:, at] += q[2 * k : 2 * k + 2]


def bf16(*shape):
    return jax.ShapeDtypeStruct(shape, B)


def split_rows(v):
    high = v.astype(B).astype(F)
    return jnp.concatenate([high, v - high], axis=0).astype(B)


def split_dot(rows, matrix, dims):
    high = matrix.astype(B)
    low = (matrix - high.astype(F)).astype(B)
    v = dot(rows, high, dims) + dot(rows, low, dims)
    return v[0:8] + v[8:16]


def up_kernel(charges, basis, transfer, out):
    row = lax.broadcasted_iota(jnp.int32, (8, PTS), 0)

    def put(at, v):
        out[at : at + 1, 0:RANK] = v[0:1]
        out[at : at + 1, RANK : 2 * RANK] = v[1:2]

    current = []
    for i in range(LEAVES):
        c = charges[:, i * PTS : (i + 1) * PTS]
        c = jnp.where(row == 0, c[0:1], jnp.where(row == 1, c[1:2], 0.0))
        v = split_dot(split_rows(c), basis[i], NT)
        put(i, v)
        current.append(v)
    for level in range(1, 5):
        per_block = 8 >> (level - 1)
        lifted = [
            dot_hi(v, transfer[d // per_block, TRANSFER_OFFSETS[level - 1] + d % per_block], NN)
            for d, v in enumerate(current)
        ]
        current = [lifted[d] + lifted[d + 1] for d in range(0, len(lifted), 2)]
        for d, v in enumerate(current):
            put(LEVEL_ROW[level] + d, v)
    out[31:32, :] = jnp.zeros((1, 2 * RANK), F)


def couple(block, rows, table, coupling, picked, products):
    picked[120:128, :] = jnp.zeros((8, 2 * RANK), F)
    for q in range(PAIRS):
        picked[q : q + 1, :] = table[pl.ds(rows[block, q], 1), :]
    turned = picked[...].T
    g = [turned[c * RANK : (c + 1) * RANK, 0:PAIRS] for c in range(2)]

    def part(n, _):
        at = pl.ds(pl.multiple_of(n * 8, 8), 8)
        b = coupling[block, at]
        for c in range(2):
            products[c, at, :] = jnp.sum(b * g[c][None], axis=1)
        return 0

    lax.fori_loop(0, RANK // 8, part, 0)
    pair = lax.broadcasted_iota(jnp.int32, (16, PAIRS), 1)
    target = lax.broadcasted_iota(jnp.int32, (16, PAIRS), 0)
    member = jnp.where(lax.shift_right_arithmetic(pair, 3) == target, 1.0, 0.0)
    return [dot_hi(member, products[c], NT) for c in range(2)]


def down_kernel(rows, own, other, coupling, transfer, basis, out, table, picked, products, held):
    half = own.shape[0]
    table[0:half, :] = own[...]
    table[half : 2 * half, :] = other[...]
    held[...] = jnp.zeros_like(held)
    for block in range(2):
        for c, t in enumerate(couple(block, rows, table, coupling, picked.at[block], products.at[block])):
            for n in range(16):
                held[16 * block + n, c : c + 1, :] = t[n : n + 1]
    current = [held[15] + held[31]]
    first = (0, 8, 12, 14)
    for level in range(4, 0, -1):
        per_block = 8 >> (level - 1)
        current = [
            held[16 * (d // per_block) + first[level - 1] + d % per_block]
            + dot_hi(
                current[d // 2],
                transfer[d // per_block, TRANSFER_OFFSETS[level - 1] + d % per_block],
                NT,
            )
            for d in range(2 * per_block)
        ]
    for i in range(LEAVES):
        v = split_dot(split_rows(current[i]), basis[i], NN)
        out[:, i * PTS : (i + 1) * PTS] = v[0:2]


def shards(coords, charges, leaf_basis, transfer, coupling, far_pairs, near_list, near_count):
    device = lax.axis_index("leaf").astype(jnp.int32)
    rhs_index = lax.axis_index("rhs").astype(jnp.int32)
    meta = jnp.stack([device * LEAVES, rhs_index])
    count = NX * NZ * NC

    def swap_rhs(v, k):
        return lax.ppermute(v, "rhs", [(i, i ^ k) for i in range(RHS)])

    def shift_leaf(v, s):
        return lax.ppermute(v, "leaf", [(d, (d + s) % count) for d in range(count)])

    first = swap_rhs(charges, 1)
    onward = jnp.concatenate([charges, first], 0)
    lists, sf, tab, place = call(
        prep_kernel,
        [
            jax.ShapeDtypeStruct((8, 128), jnp.int32),
            bf16(LEAVES, QUART, 32),
            bf16(LEAVES, 16, PTS),
            (2, LEAVES * QUART),
        ],
        [SMEM, HBM, HBM, VMEM, ANY],
        [
            pltpu.SMEM((LEAVES, NEAR), jnp.int32),
            pltpu.SMEM((LEAVES,), jnp.int32),
            pltpu.SemaphoreType.DMA((2,)),
        ],
        micros=4,
        smem_outs=1,
    )(meta, near_list, near_count, coords, onward)
    second = swap_rhs(onward, 2)
    (table,) = call(up_kernel, [(32, 2 * RANK)], [VMEM] * 3, micros=4)(
        charges, leaf_basis, transfer
    )

    acc_shape, quart_shape = (LEAVES + 1, 16, PTS), (LEAVES + 1, 16, QUART)
    values = [pltpu.VMEM((QUART, PTS), B)] * 4
    after, edges = table, None
    for w, s in enumerate(SHIFTS):
        rows = after.shape[0]
        got = shift_leaf(after if edges is None else jnp.concatenate([after, edges], 0), s)
        if w == 1:
            up, edges = got[rows : rows + EDGE], got[rows + EDGE :]
        if w == 2:
            down, edges = got[rows:], None
        data, extra, scratch = [lists, coords, tab, sf], [], [*values]
        if w == 0:
            data += [charges, first, second, place]
            extra = [bf16(LEAVES, 16, QUART), bf16(LEAVES, 16, PTS), (2 * EDGE, 128)]
        else:
            data += [cw, call_w, acc, quart]
        if w == WINDOWS - 1:
            scratch += [pltpu.VMEM(acc_shape, F), pltpu.VMEM(quart_shape, F)]
        if w == WINDOWS - 2:
            data += [down, up]
            extra = [bf16(24, QUART, 32), bf16(24, 16, QUART)]
        carried = [after] if w < WINDOWS - 1 else []
        outs = [(2, LEAVES * PTS)] * 4 if w == WINDOWS - 1 else [acc_shape, quart_shape]
        result = call(
            functools.partial(near_kernel, w, len(carried)),
            [*outs, *extra, *(v.shape for v in carried)],
            [SMEM] + [VMEM] * (len(data) + len(carried) - 1),
            scratch,
            micros=9,
        )(*data, *carried)
        if w == WINDOWS - 1:
            whole = result
            break
        acc, quart = result[:2]
        after = jnp.concatenate([result[-1], got[:rows]], 0)
        if w == 0:
            cw, call_w, edges = result[2:5]
        if w == WINDOWS - 2:
            sf, cw = result[2:4]
    other = got

    level = jnp.asarray([k for k in range(5) for _ in range(64 >> k)], jnp.int32)[None, :]
    owner = lax.shift_right_logical(far_pairs, 4 - level)
    inside = far_pairs & (lax.shift_left(jnp.int32(1), 4 - level) - 1)
    start = jnp.asarray([LEVEL_ROW[k] for k in range(5) for _ in range(64 >> k)], jnp.int32)[None, :]
    place_on = (owner - device) & (count - 1)
    bit_1 = place_on & 1
    half = lax.shift_right_logical(place_on, 1)
    bit_2 = half & 1
    fourth = lax.shift_right_logical(half + bit_2, 1)
    bit_3 = fourth & 1
    bit_0, bit_5, bit_4 = (lax.shift_right_logical(fourth, n) & 1 for n in (1, 2, 3))
    block = bit_0 + 2 * bit_1 + 4 * bit_2 + 8 * bit_3 + 16 * bit_4 + 32 * bit_5
    rows = block * 32 + start + inside
    back = [swap_rhs(whole[k], k) for k in (2, 1, 3)]
    (distant,) = call(
        down_kernel,
        [(2, LEAVES * PTS)],
        [SMEM] + [VMEM] * 5,
        [
            pltpu.VMEM((2048, 2 * RANK), F),
            pltpu.VMEM((2, 128, 2 * RANK), F),
            pltpu.VMEM((2, 2, RANK, PAIRS), F),
            pltpu.VMEM((32, 8, RANK), F),
        ],
        micros=8,
    )(rows, after, other, coupling.transpose(0, 2, 3, 1), transfer, leaf_basis)
    return distant + whole[0] + back[0] + back[1] + back[2]


def solution(mesh):
    return jax.shard_map(
        shards,
        mesh=mesh,
        in_specs=(
            P(None, "leaf"),
            P("rhs", "leaf"),
            P("leaf", None, None),
            P("leaf", None, None, None),
            P("leaf", None, None, None),
            P("leaf", None),
            P("leaf", None),
            P("leaf"),
        ),
        out_specs=P("rhs", "leaf"),
        check_vma=False,
    )
```

```python
import functools

import jax
import jax.numpy as jnp
from jax import lax
from jax.experimental import pallas as pl
from jax.experimental.pallas import tpu as pltpu
from jax.sharding import PartitionSpec as P

F = jnp.float32
B = jnp.bfloat16
NN = (((1,), (0,)), ((), ()))
NT = (((1,), (1,)), ((), ()))
HI = lax.Precision.HIGHEST

FAR = 8
STRIP = 4
LEAVES = 16
PTS = 1024
QUART = 256
RANK = 64
NEAR = 9
RHS = 4
NX, NZ, NC = 4, 8, 2
LEVEL_ROW = (0, 16, 24, 28, 30)
TRANSFER_OFFSETS = (0, 8, 12, 14)
RATE = -4.0 * 1.4426950408889634
S_LIMB = (0, 0, 1, 1, 0, 2, 1, 2)
T_LIMB = (0, 1, 0, 1, 2, 0, 2, 1)
PAIRS = 124
WINDOWS = 6
SINGLE = 80
EDGE = 128
SHIFTS = (-16, -1, 2, -8, -4, 32)
ANY = pl.BlockSpec(memory_space=pl.ANY)
HBM = pl.BlockSpec(memory_space=pltpu.HBM)
VMEM = pl.BlockSpec(memory_space=pltpu.VMEM)
SMEM = pl.BlockSpec(memory_space=pltpu.SMEM)
PARAMS = pltpu.CompilerParams(vmem_limit_bytes=24 * 2**20)


def dot(a, b, dims):
    return lax.dot_general(a, b, dims, preferred_element_type=F)


def dot_hi(a, b, dims):
    return lax.dot_general(a, b, dims, preferred_element_type=F, precision=HI)


def call(kernel, outs, in_specs, scratch=(), micros=1.0, smem_outs=0):
    outs = [v if isinstance(v, jax.ShapeDtypeStruct) else jax.ShapeDtypeStruct(v, F) for v in outs]
    return pl.pallas_call(
        kernel,
        out_shape=outs,
        in_specs=in_specs,
        out_specs=[SMEM if n < smem_outs else VMEM for n in range(len(outs))],
        scratch_shapes=list(scratch),
        compiler_params=PARAMS,
        cost_estimate=pl.CostEstimate(
            flops=int(micros * 10**9), bytes_accessed=10**5, transcendentals=0
        ),
    )


def limbs(v):
    first = v.astype(B).astype(F)
    rest = v - first
    second = rest.astype(B).astype(F)
    return first, second, rest - second


def pick(row, values, rest):
    out = rest
    for n, v in reversed(list(enumerate(values))):
        out = jnp.where(row == n, v, out)
    return out


def source_rows(x, y):
    shape = (8, x.shape[1])
    row = lax.broadcasted_iota(jnp.int32, shape, 0)
    x, y = jnp.broadcast_to(x, shape), jnp.broadcast_to(y, shape)
    lx, ly, ls = limbs(-2.0 * x), limbs(-2.0 * y), limbs(x * x + y * y)
    zero = jnp.zeros(shape, F)
    one = zero + 1.0
    return jnp.concatenate(
        [
            pick(row, [lx[a] for a in S_LIMB], zero),
            pick(row, [ly[a] for a in S_LIMB], zero),
            pick(row, [one, one, one, *ls], zero),
            pick(row, [*lx, *ly], zero),
        ],
        axis=0,
    )


def target_rows(x, y):
    shape = (8, x.shape[1])
    row = lax.broadcasted_iota(jnp.int32, shape, 0)
    lx, ly = (limbs(jnp.broadcast_to(v, shape)) for v in (x, y))
    zero = jnp.zeros(shape, F)
    return jnp.concatenate(
        [pick(row, [lx[b] for b in T_LIMB], zero), pick(row, [ly[b] for b in T_LIMB], zero)], axis=0
    ).astype(B)


def prep_kernel(meta, list_hbm, count_hbm, coords, _, lists, sf, tab, place, near_list, near_count, sems):
    copies = [
        pltpu.make_async_copy(list_hbm, near_list, sems.at[0]),
        pltpu.make_async_copy(count_hbm, near_count, sems.at[1]),
    ]
    for copy in copies:
        copy.start()
    first, r = meta[0], meta[1]
    for i in range(LEAVES):
        source = pl.ds(pl.multiple_of(r * QUART + i * PTS, QUART), QUART)
        place[:, i * QUART : (i + 1) * QUART] = coords[:, source]
    for n in range(4):
        xy = place[:, 4 * n * QUART : 4 * (n + 1) * QUART] - 0.5
        put_sources(xy, sf, 4 * n)
    for i in range(LEAVES):
        xy = coords[:, i * PTS : (i + 1) * PTS] - 0.5
        tab[i] = target_rows(xy[0:1], xy[1:2])
    for copy in copies:
        copy.wait()

    def put(p, *values):
        for field, value in zip((0, 1, 2, 3, 4, 6), values):
            lists[field, p] = value

    def leaf_pairs(i, counts):
        def slot(s, counts):
            local = near_list[i, s] - first
            before, after = local < 0, local >= LEAVES
            over = (before | after).astype(jnp.int32)
            both = 1 - over
            same = (local == i).astype(jnp.int32)
            later = (local > i).astype(jnp.int32) * both
            p = jnp.where(over == 1, SINGLE + LEAVES + counts[1], counts[0])
            p = jnp.where(same == 1, SINGLE + i, p)

            @pl.when(over + same + later > 0)
            def _():
                put(
                    p,
                    i,
                    jnp.where(before, local + 20, jnp.where(after, local + 4, local)),
                    i,
                    lax.shift_right_arithmetic(local, 2) - lax.shift_right_arithmetic(i, 2),
                    (local & 3) - (i & 3),
                    local,
                )

            return counts[0] + later, counts[1] + over

        return lax.fori_loop(0, near_count[i], slot, counts)

    twice, over = lax.fori_loop(0, LEAVES, leaf_pairs, (jnp.int32(0), jnp.int32(0)))
    put(twice, 0, 0, LEAVES, 0, 0, LEAVES)
    for p in range(4):
        put(SINGLE + LEAVES + over + p, 0, 0, LEAVES, 0, 0, LEAVES)
    lists[5, 0] = (twice + 1) & -2
    lists[5, 1] = LEAVES + over
    lists[5, 2] = r


def put_sources(xy, sf, at):
    rows = source_rows(xy[0:1], xy[1:2])
    rows = jnp.concatenate([rows[:, n * QUART : (n + 1) * QUART] for n in range(4)], axis=0)
    turned = rows.T
    for n in range(4):
        sf[at + n] = turned[:, n * 32 : (n + 1) * 32].astype(B)


def weights(c):
    high = c.astype(B).astype(F)
    return jnp.concatenate([high, c - high], axis=0).astype(B)


def near_kernel(w, n_carried, *refs):
    refs = list(refs)

    def take(n):
        taken = refs[:n]
        del refs[:n]
        return taken

    last = w == WINDOWS - 1
    lists, coords, tab, sf = take(4)
    if w == 0:
        own, first, second, place = take(4)
    else:
        cw, call_w, acc_in, quart_in = take(4)
    if w == WINDOWS - 2:
        halos = take(2)
    carried = take(n_carried)
    outs = take(4 if last else 2)
    if w == 0:
        cw, call_w, payload = take(3)
    if w == WINDOWS - 2:
        sf_own, cw_own = sf, cw
        sf, cw = take(2)
    for ref, out in zip(carried, take(n_carried)):
        out[...] = ref[...]
    kh_a, kl_a, kh_b, kl_b = take(4)
    acc, quart = take(2) if last else outs
    r = lists[5, 2]
    mine = pl.ds(pl.multiple_of(r * QUART, QUART), QUART)

    if w == 0:
        for j in range(LEAVES):
            at = slice(j * PTS, (j + 1) * PTS)
            call_w[j] = weights(jnp.concatenate([own[:, at], first[:, at], second[:, at]], axis=0))
            cw[j] = call_w[j, :, mine]
        payload[...] = jnp.zeros_like(payload)
        for end, start in enumerate((0, 12)):
            for m in range(8):
                top = end * EDGE + 16 * m
                at = (start + m // 2) * QUART + m % 2 * 128
                payload[top : top + 2] = place[:, at : at + 128]
                at = r * QUART + (start + m // 2) * PTS + m % 2 * 128
                source = pl.ds(pl.multiple_of(at, 128), 128)
                payload[top + 2 : top + 4] = own[:, source]
                payload[top + 4 : top + 6] = first[:, source]
                payload[top + 6 : top + 10] = second[:, source]
        acc[...] = jnp.zeros_like(acc)
        quart[...] = jnp.zeros_like(quart)
    else:
        acc[...] = acc_in[...]
        quart[...] = quart_in[...]
    if w == WINDOWS - 2:
        sf[0:LEAVES] = sf_own[...]
        cw[0:LEAVES] = cw_own[...]
        for n, halo in enumerate(halos):
            halo = jnp.concatenate([halo[16 * m : 16 * m + 10] for m in range(8)], axis=1)
            put_sources(halo[0:2] - 0.5, sf, LEAVES + 4 * n)
            for j in range(4):
                cw[LEAVES + 4 * n + j] = weights(halo[2:10, j * QUART : (j + 1) * QUART])

    n_twice, n_single = lists[5, 0], lists[5, 1]

    def bounds(n):
        if n == 0:
            return jnp.int32(0), jnp.int32(0)
        if n == WINDOWS:
            return n_twice, n_single
        at = lax.div((3 * n_twice + 2 * n_single) * n, WINDOWS)
        here = n_single if n > WINDOWS - 2 else LEAVES
        single = jnp.maximum(lax.shift_right_arithmetic(at - 3 * n_twice, 1), 0)
        return jnp.minimum(n_twice, lax.div(at, 3)) & -2, jnp.minimum(here, single) & -2

    (twice_0, single_0), (twice_1, single_1) = bounds(w), bounds(w + 1)

    row = lax.broadcasted_iota(jnp.int32, (8, PTS), 0)
    low, middle = row < 3, (row >= 3) & (row < 6)
    ones = jnp.where(middle, 1.0, 0.0)

    def evaluate(p, kh, kl):
        i, j = lists[0, p], lists[1, p]
        ox, oy = lists[3, p].astype(F), lists[4, p].astype(F)
        xy = coords[:, pl.ds(pl.multiple_of(i * PTS, PTS), PTS)] - 0.5
        x = jnp.broadcast_to(xy[0:1], (8, PTS)) - ox
        y = jnp.broadcast_to(xy[1:2], (8, PTS)) - oy
        ls = limbs(x * x + y * y)
        squares = pick(row, ls, ones)
        offsets = jnp.where(low, -ox, jnp.where(middle, -oy, 0.0))
        t_rows = jnp.concatenate(
            [tab[i], jnp.concatenate([squares, offsets], axis=0).astype(B)], axis=0
        )
        s_rows = sf[j]
        for c in range(4):
            lanes = slice(c * 256, (c + 1) * 256)
            dist2 = dot(s_rows, t_rows[:, lanes], NN)
            for g in range(16):
                at = slice(g * 16, (g + 1) * 16)
                d2 = jnp.maximum(dist2[at], 1e-35)
                k = jnp.exp2((d2 * lax.rsqrt(d2)) * RATE)
                high = k.astype(B)
                kh[at, lanes] = high
                kl[at, lanes] = (k - high.astype(F)).astype(B)

    def multiply(p, kh, kl, both, none=False):
        i, j = lists[0, p], lists[1, p]
        high, low_part = kh[...], kl[...]
        to = jnp.where(none, LEAVES, lists[2, p])
        acc[to] += dot(cw[j], high, NN) + dot(cw[j], low_part, NN)
        if both:
            to = jnp.where(none, LEAVES, lists[6, p])
            quart[to] += dot(call_w[i], high, NT) + dot(call_w[i], low_part, NT)

    def run(begin, end, both):
        def step(n, _):
            p = begin + 2 * n
            evaluate(p, kh_a, kl_a)
            multiply(jnp.maximum(p - 1, begin), kh_b, kl_b, both, n == 0)
            evaluate(p + 1, kh_b, kl_b)
            multiply(p, kh_a, kl_a, both)
            return 0

        steps = (end - begin + 1) // 2

        @pl.when(steps > 0)
        def _():
            lax.fori_loop(0, steps, step, 0)
            multiply(begin + 2 * steps - 1, kh_b, kl_b, both)

    run(twice_0, twice_1, True)
    run(single_0 + SINGLE, single_1 + SINGLE, False)

    if last:
        for i in range(LEAVES):
            v = (acc[i, 0:8, :] + acc[i, 8:16, :]) * (PTS**-0.5)
            for k in range(RHS):
                outs[k][:, i * PTS : (i + 1) * PTS] = v[2 * k : 2 * k + 2]
            q = (quart[i, 0:8, :] + quart[i, 8:16, :]) * (PTS**-0.5)
            at = pl.ds(pl.multiple_of(r * QUART + i * PTS, QUART), QUART)
            for k in range(RHS):
                outs[k][:, at] += q[2 * k : 2 * k + 2]


def bf16(*shape):
    return jax.ShapeDtypeStruct(shape, B)


def split_rows(v):
    high = v.astype(B).astype(F)
    return jnp.concatenate([high, v - high], axis=0).astype(B)


def split_dot(rows, matrix, dims):
    high = matrix.astype(B)
    low = (matrix - high.astype(F)).astype(B)
    v = dot(rows, high, dims) + dot(rows, low, dims)
    return v[0:8] + v[8:16]


def up_kernel(charges, basis, transfer, out):
    row = lax.broadcasted_iota(jnp.int32, (8, PTS), 0)

    def put(at, v):
        out[at : at + 1, 0:RANK] = v[0:1]
        out[at : at + 1, RANK : 2 * RANK] = v[1:2]

    current = []
    for i in range(LEAVES):
        c = charges[:, i * PTS : (i + 1) * PTS]
        c = jnp.where(row == 0, c[0:1], jnp.where(row == 1, c[1:2], 0.0))
        v = split_dot(split_rows(c), basis[i], NT)
        put(i, v)
        current.append(v)
    for level in range(1, 5):
        per_block = 8 >> (level - 1)
        lifted = [
            dot_hi(v, transfer[d // per_block, TRANSFER_OFFSETS[level - 1] + d % per_block], NN)
            for d, v in enumerate(current)
        ]
        current = [lifted[d] + lifted[d + 1] for d in range(0, len(lifted), 2)]
        for d, v in enumerate(current):
            put(LEVEL_ROW[level] + d, v)
    out[31:32, :] = jnp.zeros((1, 2 * RANK), F)


def couple(block, rows, table, coupling, picked, products):
    picked[120:128, :] = jnp.zeros((8, 2 * RANK), F)
    for q in range(PAIRS):
        picked[q : q + 1, :] = table[pl.ds(rows[block, q], 1), :]
    turned = picked[...].T
    g = [turned[c * RANK : (c + 1) * RANK, 0:PAIRS] for c in range(2)]

    def part(n, _):
        at = pl.ds(pl.multiple_of(n * 8, 8), 8)
        b = coupling[block, at]
        for c in range(2):
            products[c, at, :] = jnp.sum(b * g[c][None], axis=1)
        return 0

    lax.fori_loop(0, RANK // 8, part, 0)
    pair = lax.broadcasted_iota(jnp.int32, (16, PAIRS), 1)
    target = lax.broadcasted_iota(jnp.int32, (16, PAIRS), 0)
    member = jnp.where(lax.shift_right_arithmetic(pair, 3) == target, 1.0, 0.0)
    return [dot_hi(member, products[c], NT) for c in range(2)]


def down_kernel(rows, own, other, coupling, transfer, basis, out, table, picked, products, held):
    half = own.shape[0]
    table[0:half, :] = own[...]
    table[half : 2 * half, :] = other[...]
    held[...] = jnp.zeros_like(held)
    for block in range(2):
        for c, t in enumerate(couple(block, rows, table, coupling, picked.at[block], products.at[block])):
            for n in range(16):
                held[16 * block + n, c : c + 1, :] = t[n : n + 1]
    current = [held[15] + held[31]]
    first = (0, 8, 12, 14)
    for level in range(4, 0, -1):
        per_block = 8 >> (level - 1)
        current = [
            held[16 * (d // per_block) + first[level - 1] + d % per_block]
            + dot_hi(
                current[d // 2],
                transfer[d // per_block, TRANSFER_OFFSETS[level - 1] + d % per_block],
                NT,
            )
            for d in range(2 * per_block)
        ]
    for i in range(LEAVES):
        v = split_dot(split_rows(current[i]), basis[i], NN)
        out[:, i * PTS : (i + 1) * PTS] = v[0:2]


def shards(coords, charges, leaf_basis, transfer, coupling, far_pairs, near_list, near_count):
    device = lax.axis_index("leaf").astype(jnp.int32)
    rhs_index = lax.axis_index("rhs").astype(jnp.int32)
    meta = jnp.stack([device * LEAVES, rhs_index])
    count = NX * NZ * NC

    def swap_rhs(v, k):
        return lax.ppermute(v, "rhs", [(i, i ^ k) for i in range(RHS)])

    def shift_leaf(v, s):
        return lax.ppermute(v, "leaf", [(d, (d + s) % count) for d in range(count)])

    first = swap_rhs(charges, 1)
    onward = jnp.concatenate([charges, first], 0)
    lists, sf, tab, place = call(
        prep_kernel,
        [
            jax.ShapeDtypeStruct((8, 128), jnp.int32),
            bf16(LEAVES, QUART, 32),
            bf16(LEAVES, 16, PTS),
            (2, LEAVES * QUART),
        ],
        [SMEM, HBM, HBM, VMEM, ANY],
        [
            pltpu.SMEM((LEAVES, NEAR), jnp.int32),
            pltpu.SMEM((LEAVES,), jnp.int32),
            pltpu.SemaphoreType.DMA((2,)),
        ],
        micros=4,
        smem_outs=1,
    )(meta, near_list, near_count, coords, onward)
    second = swap_rhs(onward, 2)
    (table,) = call(up_kernel, [(32, 2 * RANK)], [VMEM] * 3, micros=4)(
        charges, leaf_basis, transfer
    )

    acc_shape, quart_shape = (LEAVES + 1, 16, PTS), (LEAVES + 1, 16, QUART)
    values = [pltpu.VMEM((QUART, PTS), B)] * 4
    after, edges = table, None
    for w, s in enumerate(SHIFTS):
        rows = after.shape[0]
        got = shift_leaf(after if edges is None else jnp.concatenate([after, edges], 0), s)
        if w == 1:
            up, edges = got[rows : rows + EDGE], got[rows + EDGE :]
        if w == 2:
            down, edges = got[rows:], None
        data, extra, scratch = [lists, coords, tab, sf], [], [*values]
        if w == 0:
            data += [charges, first, second, place]
            extra = [bf16(LEAVES, 16, QUART), bf16(LEAVES, 16, PTS), (2 * EDGE, 128)]
        else:
            data += [cw, call_w, acc, quart]
        if w == WINDOWS - 1:
            scratch += [pltpu.VMEM(acc_shape, F), pltpu.VMEM(quart_shape, F)]
        if w == WINDOWS - 2:
            data += [down, up]
            extra = [bf16(24, QUART, 32), bf16(24, 16, QUART)]
        carried = [after] if w < WINDOWS - 1 else []
        outs = [(2, LEAVES * PTS)] * 4 if w == WINDOWS - 1 else [acc_shape, quart_shape]
        result = call(
            functools.partial(near_kernel, w, len(carried)),
            [*outs, *extra, *(v.shape for v in carried)],
            [SMEM] + [VMEM] * (len(data) + len(carried) - 1),
            scratch,
            micros=9,
        )(*data, *carried)
        if w == WINDOWS - 1:
            whole = result
            break
        acc, quart = result[:2]
        after = jnp.concatenate([result[-1], got[:rows]], 0)
        if w == 0:
            cw, call_w, edges = result[2:5]
        if w == WINDOWS - 2:
            sf, cw = result[2:4]
    other = got

    level = jnp.asarray([k for k in range(5) for _ in range(64 >> k)], jnp.int32)[None, :]
    owner = lax.shift_right_logical(far_pairs, 4 - level)
    inside = far_pairs & (lax.shift_left(jnp.int32(1), 4 - level) - 1)
    start = jnp.asarray([LEVEL_ROW[k] for k in range(5) for _ in range(64 >> k)], jnp.int32)[None, :]
    place_on = (owner - device) & (count - 1)
    bit_1 = place_on & 1
    half = lax.shift_right_logical(place_on, 1)
    bit_2 = half & 1
    fourth = lax.shift_right_logical(half + bit_2, 1)
    bit_4, bit_3, bit_0, bit_5 = (lax.shift_right_logical(fourth, n) & 1 for n in range(4))
    block = bit_0 + 2 * bit_1 + 4 * bit_2 + 8 * bit_3 + 16 * bit_4 + 32 * bit_5
    rows = block * 32 + start + inside
    back = [swap_rhs(whole[k], k) for k in (2, 1, 3)]
    (distant,) = call(
        down_kernel,
        [(2, LEAVES * PTS)],
        [SMEM] + [VMEM] * 5,
        [
            pltpu.VMEM((2048, 2 * RANK), F),
            pltpu.VMEM((2, 128, 2 * RANK), F),
            pltpu.VMEM((2, 2, RANK, PAIRS), F),
            pltpu.VMEM((32, 8, RANK), F),
        ],
        micros=8,
    )(rows, after, other, coupling.transpose(0, 2, 3, 1), transfer, leaf_basis)
    return distant + whole[0] + back[0] + back[1] + back[2]


def solution(mesh):
    return jax.shard_map(
        shards,
        mesh=mesh,
        in_specs=(
            P(None, "leaf"),
            P("rhs", "leaf"),
            P("leaf", None, None),
            P("leaf", None, None, None),
            P("leaf", None, None, None),
            P("leaf", None),
            P("leaf", None),
            P("leaf"),
        ),
        out_specs=P("rhs", "leaf"),
        check_vma=False,
    )
```

```python
import functools

import jax
import jax.numpy as jnp
from jax import lax
from jax.experimental import pallas as pl
from jax.experimental.pallas import tpu as pltpu
from jax.sharding import PartitionSpec as P

F = jnp.float32
B = jnp.bfloat16
NN = (((1,), (0,)), ((), ()))
NT = (((1,), (1,)), ((), ()))
HI = lax.Precision.HIGHEST

FAR = 8
STRIP = 4
LEAVES = 16
PTS = 1024
QUART = 256
RANK = 64
NEAR = 9
RHS = 4
NX, NZ, NC = 4, 8, 2
LEVEL_ROW = (0, 16, 24, 28, 30)
TRANSFER_OFFSETS = (0, 8, 12, 14)
RATE = -4.0 * 1.4426950408889634
S_LIMB = (0, 0, 1, 1, 0, 2, 1, 2)
T_LIMB = (0, 1, 0, 1, 2, 0, 2, 1)
PAIRS = 124
WINDOWS = 6
SINGLE = 80
EDGE = 128
SWAP = 8
SHIFTS = (0, -1, 2, -4, 32, -16)
ANY = pl.BlockSpec(memory_space=pl.ANY)
HBM = pl.BlockSpec(memory_space=pltpu.HBM)
VMEM = pl.BlockSpec(memory_space=pltpu.VMEM)
SMEM = pl.BlockSpec(memory_space=pltpu.SMEM)
PARAMS = pltpu.CompilerParams(vmem_limit_bytes=24 * 2**20)


def dot(a, b, dims):
    return lax.dot_general(a, b, dims, preferred_element_type=F)


def dot_hi(a, b, dims):
    return lax.dot_general(a, b, dims, preferred_element_type=F, precision=HI)


def call(kernel, outs, in_specs, scratch=(), micros=1.0, smem_outs=0):
    outs = [v if isinstance(v, jax.ShapeDtypeStruct) else jax.ShapeDtypeStruct(v, F) for v in outs]
    return pl.pallas_call(
        kernel,
        out_shape=outs,
        in_specs=in_specs,
        out_specs=[SMEM if n < smem_outs else VMEM for n in range(len(outs))],
        scratch_shapes=list(scratch),
        compiler_params=PARAMS,
        cost_estimate=pl.CostEstimate(
            flops=int(micros * 10**9), bytes_accessed=10**5, transcendentals=0
        ),
    )


def limbs(v):
    first = v.astype(B).astype(F)
    rest = v - first
    second = rest.astype(B).astype(F)
    return first, second, rest - second


def pick(row, values, rest):
    out = rest
    for n, v in reversed(list(enumerate(values))):
        out = jnp.where(row == n, v, out)
    return out


def source_rows(x, y):
    shape = (8, x.shape[1])
    row = lax.broadcasted_iota(jnp.int32, shape, 0)
    x, y = jnp.broadcast_to(x, shape), jnp.broadcast_to(y, shape)
    lx, ly, ls = limbs(-2.0 * x), limbs(-2.0 * y), limbs(x * x + y * y)
    zero = jnp.zeros(shape, F)
    one = zero + 1.0
    return jnp.concatenate(
        [
            pick(row, [lx[a] for a in S_LIMB], zero),
            pick(row, [ly[a] for a in S_LIMB], zero),
            pick(row, [one, one, one, *ls], zero),
            pick(row, [*lx, *ly], zero),
        ],
        axis=0,
    )


def target_rows(x, y):
    shape = (8, x.shape[1])
    row = lax.broadcasted_iota(jnp.int32, shape, 0)
    lx, ly = (limbs(jnp.broadcast_to(v, shape)) for v in (x, y))
    zero = jnp.zeros(shape, F)
    return jnp.concatenate(
        [pick(row, [lx[b] for b in T_LIMB], zero), pick(row, [ly[b] for b in T_LIMB], zero)], axis=0
    ).astype(B)


def prep_kernel(meta, list_hbm, count_hbm, coords, _, lists, sf, tab, place, near_list, near_count, sems):
    copies = [
        pltpu.make_async_copy(list_hbm, near_list, sems.at[0]),
        pltpu.make_async_copy(count_hbm, near_count, sems.at[1]),
    ]
    for copy in copies:
        copy.start()
    first, r = meta[0], meta[1]
    for i in range(LEAVES):
        source = pl.ds(pl.multiple_of(r * QUART + i * PTS, QUART), QUART)
        place[:, i * QUART : (i + 1) * QUART] = coords[:, source]
    for n in range(4):
        xy = place[:, 4 * n * QUART : 4 * (n + 1) * QUART] - 0.5
        put_sources(xy, sf, 4 * n)
    for i in range(LEAVES):
        xy = coords[:, i * PTS : (i + 1) * PTS] - 0.5
        tab[i] = target_rows(xy[0:1], xy[1:2])
    for copy in copies:
        copy.wait()

    def put(p, *values):
        for field, value in zip((0, 1, 2, 3, 4, 6), values):
            lists[field, p] = value

    def leaf_pairs(i, counts):
        def slot(s, counts):
            local = near_list[i, s] - first
            before, after = local < 0, local >= LEAVES
            over = (before | after).astype(jnp.int32)
            both = 1 - over
            same = (local == i).astype(jnp.int32)
            later = (local > i).astype(jnp.int32) * both
            p = jnp.where(over == 1, SINGLE + LEAVES + counts[1], counts[0])
            p = jnp.where(same == 1, SINGLE + i, p)

            @pl.when(over + same + later > 0)
            def _():
                put(
                    p,
                    i,
                    jnp.where(before, local + 20, jnp.where(after, local + 4, local)),
                    i,
                    lax.shift_right_arithmetic(local, 2) - lax.shift_right_arithmetic(i, 2),
                    (local & 3) - (i & 3),
                    local,
                )

            return counts[0] + later, counts[1] + over

        return lax.fori_loop(0, near_count[i], slot, counts)

    twice, over = lax.fori_loop(0, LEAVES, leaf_pairs, (jnp.int32(0), jnp.int32(0)))
    put(twice, 0, 0, LEAVES, 0, 0, LEAVES)
    for p in range(4):
        put(SINGLE + LEAVES + over + p, 0, 0, LEAVES, 0, 0, LEAVES)
    lists[5, 0] = (twice + 1) & -2
    lists[5, 1] = LEAVES + over
    lists[5, 2] = r


def put_sources(xy, sf, at):
    rows = source_rows(xy[0:1], xy[1:2])
    rows = jnp.concatenate([rows[:, n * QUART : (n + 1) * QUART] for n in range(4)], axis=0)
    turned = rows.T
    for n in range(4):
        sf[at + n] = turned[:, n * 32 : (n + 1) * 32].astype(B)


def weights(c):
    high = c.astype(B).astype(F)
    return jnp.concatenate([high, c - high], axis=0).astype(B)


def near_kernel(w, n_carried, *refs):
    refs = list(refs)

    def take(n):
        taken = refs[:n]
        del refs[:n]
        return taken

    last = w == WINDOWS - 1
    lists, coords, tab, sf = take(4)
    if w == 0:
        own, first, second, place = take(4)
    else:
        cw, call_w, acc_in, quart_in = take(4)
    if w == WINDOWS - 2:
        halos = take(2)
    carried = take(n_carried)
    outs = take(4 if last else 2)
    if w == 0:
        cw, call_w, payload = take(3)
    if w == WINDOWS - 2:
        sf_own, cw_own = sf, cw
        sf, cw = take(2)
    for ref, out in zip(carried, take(n_carried)):
        out[...] = ref[...]
    kh_a, kl_a, kh_b, kl_b = take(4)
    acc, quart = take(2) if last else outs
    r = lists[5, 2]
    mine = pl.ds(pl.multiple_of(r * QUART, QUART), QUART)

    if w == 0:
        for j in range(LEAVES):
            at = slice(j * PTS, (j + 1) * PTS)
            call_w[j] = weights(jnp.concatenate([own[:, at], first[:, at], second[:, at]], axis=0))
            cw[j] = call_w[j, :, mine]
        payload[...] = jnp.zeros_like(payload)
        for end, start in enumerate((0, 12)):
            for m in range(8):
                top = end * EDGE + 16 * m
                at = (start + m // 2) * QUART + m % 2 * 128
                payload[top : top + 2] = place[:, at : at + 128]
                at = r * QUART + (start + m // 2) * PTS + m % 2 * 128
                source = pl.ds(pl.multiple_of(at, 128), 128)
                payload[top + 2 : top + 4] = own[:, source]
                payload[top + 4 : top + 6] = first[:, source]
                payload[top + 6 : top + 10] = second[:, source]
        acc[...] = jnp.zeros_like(acc)
        quart[...] = jnp.zeros_like(quart)
    else:
        acc[...] = acc_in[...]
        quart[...] = quart_in[...]
    if w == WINDOWS - 2:
        sf[0:LEAVES] = sf_own[...]
        cw[0:LEAVES] = cw_own[...]
        for n, halo in enumerate(halos):
            halo = jnp.concatenate([halo[16 * m : 16 * m + 10] for m in range(8)], axis=1)
            put_sources(halo[0:2] - 0.5, sf, LEAVES + 4 * n)
            for j in range(4):
                cw[LEAVES + 4 * n + j] = weights(halo[2:10, j * QUART : (j + 1) * QUART])

    n_twice, n_single = lists[5, 0], lists[5, 1]

    def bounds(n):
        if n == 0:
            return jnp.int32(0), jnp.int32(0)
        if n == WINDOWS:
            return n_twice, n_single
        at = lax.div((3 * n_twice + 2 * n_single) * n, WINDOWS)
        here = n_single if n > WINDOWS - 2 else LEAVES
        single = jnp.maximum(lax.shift_right_arithmetic(at - 3 * n_twice, 1), 0)
        return jnp.minimum(n_twice, lax.div(at, 3)) & -2, jnp.minimum(here, single) & -2

    (twice_0, single_0), (twice_1, single_1) = bounds(w), bounds(w + 1)

    row = lax.broadcasted_iota(jnp.int32, (8, PTS), 0)
    low, middle = row < 3, (row >= 3) & (row < 6)
    ones = jnp.where(middle, 1.0, 0.0)

    def evaluate(p, kh, kl):
        i, j = lists[0, p], lists[1, p]
        ox, oy = lists[3, p].astype(F), lists[4, p].astype(F)
        xy = coords[:, pl.ds(pl.multiple_of(i * PTS, PTS), PTS)] - 0.5
        x = jnp.broadcast_to(xy[0:1], (8, PTS)) - ox
        y = jnp.broadcast_to(xy[1:2], (8, PTS)) - oy
        ls = limbs(x * x + y * y)
        squares = pick(row, ls, ones)
        offsets = jnp.where(low, -ox, jnp.where(middle, -oy, 0.0))
        t_rows = jnp.concatenate(
            [tab[i], jnp.concatenate([squares, offsets], axis=0).astype(B)], axis=0
        )
        s_rows = sf[j]
        for c in range(4):
            lanes = slice(c * 256, (c + 1) * 256)
            dist2 = dot(s_rows, t_rows[:, lanes], NN)
            for g in range(16):
                at = slice(g * 16, (g + 1) * 16)
                d2 = jnp.maximum(dist2[at], 1e-35)
                k = jnp.exp2((d2 * lax.rsqrt(d2)) * RATE)
                high = k.astype(B)
                kh[at, lanes] = high
                kl[at, lanes] = (k - high.astype(F)).astype(B)

    def multiply(p, kh, kl, both, none=False):
        i, j = lists[0, p], lists[1, p]
        high, low_part = kh[...], kl[...]
        to = jnp.where(none, LEAVES, lists[2, p])
        acc[to] += dot(cw[j], high, NN) + dot(cw[j], low_part, NN)
        if both:
            to = jnp.where(none, LEAVES, lists[6, p])
            quart[to] += dot(call_w[i], high, NT) + dot(call_w[i], low_part, NT)

    def run(begin, end, both):
        def step(n, _):
            p = begin + 2 * n
            evaluate(p, kh_a, kl_a)
            multiply(jnp.maximum(p - 1, begin), kh_b, kl_b, both, n == 0)
            evaluate(p + 1, kh_b, kl_b)
            multiply(p, kh_a, kl_a, both)
            return 0

        steps = (end - begin + 1) // 2

        @pl.when(steps > 0)
        def _():
            lax.fori_loop(0, steps, step, 0)
            multiply(begin + 2 * steps - 1, kh_b, kl_b, both)

    run(twice_0, twice_1, True)
    run(single_0 + SINGLE, single_1 + SINGLE, False)

    if last:
        for i in range(LEAVES):
            v = (acc[i, 0:8, :] + acc[i, 8:16, :]) * (PTS**-0.5)
            for k in range(RHS):
                outs[k][:, i * PTS : (i + 1) * PTS] = v[2 * k : 2 * k + 2]
            q = (quart[i, 0:8, :] + quart[i, 8:16, :]) * (PTS**-0.5)
            at = pl.ds(pl.multiple_of(r * QUART + i * PTS, QUART), QUART)
            for k in range(RHS):
                outs[k][:, at] += q[2 * k : 2 * k + 2]


def bf16(*shape):
    return jax.ShapeDtypeStruct(shape, B)


def split_rows(v):
    high = v.astype(B).astype(F)
    return jnp.concatenate([high, v - high], axis=0).astype(B)


def split_dot(rows, matrix, dims):
    high = matrix.astype(B)
    low = (matrix - high.astype(F)).astype(B)
    v = dot(rows, high, dims) + dot(rows, low, dims)
    return v[0:8] + v[8:16]


def up_kernel(charges, basis, transfer, out):
    row = lax.broadcasted_iota(jnp.int32, (8, PTS), 0)

    def put(at, v):
        out[at : at + 1, 0:RANK] = v[0:1]
        out[at : at + 1, RANK : 2 * RANK] = v[1:2]

    current = []
    for i in range(LEAVES):
        c = charges[:, i * PTS : (i + 1) * PTS]
        c = jnp.where(row == 0, c[0:1], jnp.where(row == 1, c[1:2], 0.0))
        v = split_dot(split_rows(c), basis[i], NT)
        put(i, v)
        current.append(v)
    for level in range(1, 5):
        per_block = 8 >> (level - 1)
        lifted = [
            dot_hi(v, transfer[d // per_block, TRANSFER_OFFSETS[level - 1] + d % per_block], NN)
            for d, v in enumerate(current)
        ]
        current = [lifted[d] + lifted[d + 1] for d in range(0, len(lifted), 2)]
        for d, v in enumerate(current):
            put(LEVEL_ROW[level] + d, v)
    out[31:32, :] = jnp.zeros((1, 2 * RANK), F)


def couple(block, rows, table, coupling, picked, products):
    picked[120:128, :] = jnp.zeros((8, 2 * RANK), F)
    for q in range(PAIRS):
        picked[q : q + 1, :] = table[pl.ds(rows[block, q], 1), :]
    turned = picked[...].T
    g = [turned[c * RANK : (c + 1) * RANK, 0:PAIRS] for c in range(2)]

    def part(n, _):
        at = pl.ds(pl.multiple_of(n * 8, 8), 8)
        b = coupling[block, at]
        for c in range(2):
            products[c, at, :] = jnp.sum(b * g[c][None], axis=1)
        return 0

    lax.fori_loop(0, RANK // 8, part, 0)
    pair = lax.broadcasted_iota(jnp.int32, (16, PAIRS), 1)
    target = lax.broadcasted_iota(jnp.int32, (16, PAIRS), 0)
    member = jnp.where(lax.shift_right_arithmetic(pair, 3) == target, 1.0, 0.0)
    return [dot_hi(member, products[c], NT) for c in range(2)]


def down_kernel(rows, own, other, coupling, transfer, basis, out, table, picked, products, held):
    half = own.shape[0]
    table[0:half, :] = own[...]
    table[half : 2 * half, :] = other[...]
    held[...] = jnp.zeros_like(held)
    for block in range(2):
        for c, t in enumerate(couple(block, rows, table, coupling, picked.at[block], products.at[block])):
            for n in range(16):
                held[16 * block + n, c : c + 1, :] = t[n : n + 1]
    current = [held[15] + held[31]]
    first = (0, 8, 12, 14)
    for level in range(4, 0, -1):
        per_block = 8 >> (level - 1)
        current = [
            held[16 * (d // per_block) + first[level - 1] + d % per_block]
            + dot_hi(
                current[d // 2],
                transfer[d // per_block, TRANSFER_OFFSETS[level - 1] + d % per_block],
                NT,
            )
            for d in range(2 * per_block)
        ]
    for i in range(LEAVES):
        v = split_dot(split_rows(current[i]), basis[i], NN)
        out[:, i * PTS : (i + 1) * PTS] = v[0:2]


def shards(coords, charges, leaf_basis, transfer, coupling, far_pairs, near_list, near_count):
    device = lax.axis_index("leaf").astype(jnp.int32)
    rhs_index = lax.axis_index("rhs").astype(jnp.int32)
    meta = jnp.stack([device * LEAVES, rhs_index])
    count = NX * NZ * NC

    def swap_rhs(v, k):
        return lax.ppermute(v, "rhs", [(i, i ^ k) for i in range(RHS)])

    def shift_leaf(v, s):
        pairs = [(d, (d + s) % count if s else d ^ SWAP) for d in range(count)]
        return lax.ppermute(v, "leaf", pairs)

    first = swap_rhs(charges, 1)
    onward = jnp.concatenate([charges, first], 0)
    lists, sf, tab, place = call(
        prep_kernel,
        [
            jax.ShapeDtypeStruct((8, 128), jnp.int32),
            bf16(LEAVES, QUART, 32),
            bf16(LEAVES, 16, PTS),
            (2, LEAVES * QUART),
        ],
        [SMEM, HBM, HBM, VMEM, ANY],
        [
            pltpu.SMEM((LEAVES, NEAR), jnp.int32),
            pltpu.SMEM((LEAVES,), jnp.int32),
            pltpu.SemaphoreType.DMA((2,)),
        ],
        micros=4,
        smem_outs=1,
    )(meta, near_list, near_count, coords, onward)
    second = swap_rhs(onward, 2)
    (table,) = call(up_kernel, [(32, 2 * RANK)], [VMEM] * 3, micros=4)(
        charges, leaf_basis, transfer
    )

    acc_shape, quart_shape = (LEAVES + 1, 16, PTS), (LEAVES + 1, 16, QUART)
    values = [pltpu.VMEM((QUART, PTS), B)] * 4
    after, edges = table, None
    for w, s in enumerate(SHIFTS):
        rows = after.shape[0]
        got = shift_leaf(after if edges is None else jnp.concatenate([after, edges], 0), s)
        if w == 1:
            up, edges = got[rows : rows + EDGE], got[rows + EDGE :]
        if w == 2:
            down, edges = got[rows:], None
        data, extra, scratch = [lists, coords, tab, sf], [], [*values]
        if w == 0:
            data += [charges, first, second, place]
            extra = [bf16(LEAVES, 16, QUART), bf16(LEAVES, 16, PTS), (2 * EDGE, 128)]
        else:
            data += [cw, call_w, acc, quart]
        if w == WINDOWS - 1:
            scratch += [pltpu.VMEM(acc_shape, F), pltpu.VMEM(quart_shape, F)]
        if w == WINDOWS - 2:
            data += [down, up]
            extra = [bf16(24, QUART, 32), bf16(24, 16, QUART)]
        carried = [after] if w < WINDOWS - 1 else []
        outs = [(2, LEAVES * PTS)] * 4 if w == WINDOWS - 1 else [acc_shape, quart_shape]
        result = call(
            functools.partial(near_kernel, w, len(carried)),
            [*outs, *extra, *(v.shape for v in carried)],
            [SMEM] + [VMEM] * (len(data) + len(carried) - 1),
            scratch,
            micros=9,
        )(*data, *carried)
        if w == WINDOWS - 1:
            whole = result
            break
        acc, quart = result[:2]
        after = jnp.concatenate([result[-1], got[:rows]], 0)
        if w == 0:
            cw, call_w, edges = result[2:5]
        if w == WINDOWS - 2:
            sf, cw = result[2:4]
    other = got

    level = jnp.asarray([k for k in range(5) for _ in range(64 >> k)], jnp.int32)[None, :]
    owner = lax.shift_right_logical(far_pairs, 4 - level)
    inside = far_pairs & (lax.shift_left(jnp.int32(1), 4 - level) - 1)
    start = jnp.asarray([LEVEL_ROW[k] for k in range(5) for _ in range(64 >> k)], jnp.int32)[None, :]
    bit_0 = lax.shift_right_logical(owner - device + 2, 3) & 1
    place_on = ((owner ^ (SWAP * bit_0)) - device) & (count - 1)
    bit_1 = place_on & 1
    half = lax.shift_right_logical(place_on, 1)
    bit_2 = half & 1
    fourth = lax.shift_right_logical(half + bit_2, 1)
    bit_3, bit_5, bit_4 = (lax.shift_right_logical(fourth, n) & 1 for n in (0, 2, 3))
    block = bit_0 + 2 * bit_1 + 4 * bit_2 + 8 * bit_3 + 16 * bit_4 + 32 * bit_5
    rows = block * 32 + start + inside
    back = [swap_rhs(whole[k], k) for k in (2, 1, 3)]
    (distant,) = call(
        down_kernel,
        [(2, LEAVES * PTS)],
        [SMEM] + [VMEM] * 5,
        [
            pltpu.VMEM((2048, 2 * RANK), F),
            pltpu.VMEM((2, 128, 2 * RANK), F),
            pltpu.VMEM((2, 2, RANK, PAIRS), F),
            pltpu.VMEM((32, 8, RANK), F),
        ],
        micros=8,
    )(rows, after, other, coupling.transpose(0, 2, 3, 1), transfer, leaf_basis)
    return distant + whole[0] + back[0] + back[1] + back[2]


def solution(mesh):
    return jax.shard_map(
        shards,
        mesh=mesh,
        in_specs=(
            P(None, "leaf"),
            P("rhs", "leaf"),
            P("leaf", None, None),
            P("leaf", None, None, None),
            P("leaf", None, None, None),
            P("leaf", None),
            P("leaf", None),
            P("leaf"),
        ),
        out_specs=P("rhs", "leaf"),
        check_vma=False,
    )
```

```python
import functools

import jax
import jax.numpy as jnp
from jax import lax
from jax.experimental import pallas as pl
from jax.experimental.pallas import tpu as pltpu
from jax.sharding import PartitionSpec as P

F = jnp.float32
B = jnp.bfloat16
NN = (((1,), (0,)), ((), ()))
NT = (((1,), (1,)), ((), ()))
HI = lax.Precision.HIGHEST

FAR = 8
STRIP = 4
LEAVES = 16
PTS = 1024
QUART = 256
RANK = 64
NEAR = 9
RHS = 4
NX, NZ, NC = 4, 8, 2
LEVEL_ROW = (0, 16, 24, 28, 30)
TRANSFER_OFFSETS = (0, 8, 12, 14)
RATE = -4.0 * 1.4426950408889634
S_LIMB = (0, 0, 1, 1, 0, 2, 1, 2)
T_LIMB = (0, 1, 0, 1, 2, 0, 2, 1)
PAIRS = 124
WINDOWS = 6
SINGLE = 80
EDGE = 128
SWAP = 8
SHIFTS = (0, -1, 2, -4, 32, -16)
ANY = pl.BlockSpec(memory_space=pl.ANY)
HBM = pl.BlockSpec(memory_space=pltpu.HBM)
VMEM = pl.BlockSpec(memory_space=pltpu.VMEM)
SMEM = pl.BlockSpec(memory_space=pltpu.SMEM)
PARAMS = pltpu.CompilerParams(vmem_limit_bytes=24 * 2**20)


def dot(a, b, dims):
    return lax.dot_general(a, b, dims, preferred_element_type=F)


def dot_hi(a, b, dims):
    return lax.dot_general(a, b, dims, preferred_element_type=F, precision=HI)


def call(kernel, outs, in_specs, scratch=(), micros=1.0, smem_outs=0):
    outs = [v if isinstance(v, jax.ShapeDtypeStruct) else jax.ShapeDtypeStruct(v, F) for v in outs]
    return pl.pallas_call(
        kernel,
        out_shape=outs,
        in_specs=in_specs,
        out_specs=[SMEM if n < smem_outs else VMEM for n in range(len(outs))],
        scratch_shapes=list(scratch),
        compiler_params=PARAMS,
        cost_estimate=pl.CostEstimate(
            flops=int(micros * 10**9), bytes_accessed=10**5, transcendentals=0
        ),
    )


def limbs(v):
    first = v.astype(B).astype(F)
    rest = v - first
    second = rest.astype(B).astype(F)
    return first, second, rest - second


def pick(row, values, rest):
    out = rest
    for n, v in reversed(list(enumerate(values))):
        out = jnp.where(row == n, v, out)
    return out


def source_rows(x, y):
    shape = (8, x.shape[1])
    row = lax.broadcasted_iota(jnp.int32, shape, 0)
    x, y = jnp.broadcast_to(x, shape), jnp.broadcast_to(y, shape)
    lx, ly, ls = limbs(-2.0 * x), limbs(-2.0 * y), limbs(x * x + y * y)
    zero = jnp.zeros(shape, F)
    one = zero + 1.0
    return jnp.concatenate(
        [
            pick(row, [lx[a] for a in S_LIMB], zero),
            pick(row, [ly[a] for a in S_LIMB], zero),
            pick(row, [one, one, one, *ls], zero),
            pick(row, [*lx, *ly], zero),
        ],
        axis=0,
    )


def target_rows(x, y):
    shape = (8, x.shape[1])
    row = lax.broadcasted_iota(jnp.int32, shape, 0)
    lx, ly = (limbs(jnp.broadcast_to(v, shape)) for v in (x, y))
    zero = jnp.zeros(shape, F)
    return jnp.concatenate(
        [pick(row, [lx[b] for b in T_LIMB], zero), pick(row, [ly[b] for b in T_LIMB], zero)], axis=0
    ).astype(B)


def prep_kernel(meta, list_hbm, count_hbm, coords, _, skeleton, lists, sf, tab, place, handed, near_list, near_count, sems):
    copies = [
        pltpu.make_async_copy(list_hbm, near_list, sems.at[0]),
        pltpu.make_async_copy(count_hbm, near_count, sems.at[1]),
    ]
    for copy in copies:
        copy.start()
    handed[...] = skeleton[...]
    first, r = meta[0], meta[1]
    for i in range(LEAVES):
        source = pl.ds(pl.multiple_of(r * QUART + i * PTS, QUART), QUART)
        place[:, i * QUART : (i + 1) * QUART] = coords[:, source]
    for n in range(4):
        xy = place[:, 4 * n * QUART : 4 * (n + 1) * QUART] - 0.5
        put_sources(xy, sf, 4 * n)
    for i in range(LEAVES):
        xy = coords[:, i * PTS : (i + 1) * PTS] - 0.5
        tab[i] = target_rows(xy[0:1], xy[1:2])
    for copy in copies:
        copy.wait()

    def put(p, *values):
        for field, value in zip((0, 1, 2, 3, 4, 6), values):
            lists[field, p] = value

    def leaf_pairs(i, counts):
        def slot(s, counts):
            local = near_list[i, s] - first
            before, after = local < 0, local >= LEAVES
            over = (before | after).astype(jnp.int32)
            both = 1 - over
            same = (local == i).astype(jnp.int32)
            later = (local > i).astype(jnp.int32) * both
            p = jnp.where(over == 1, SINGLE + LEAVES + counts[1], counts[0])
            p = jnp.where(same == 1, SINGLE + i, p)

            @pl.when(over + same + later > 0)
            def _():
                put(
                    p,
                    i,
                    jnp.where(before, local + 20, jnp.where(after, local + 4, local)),
                    i,
                    lax.shift_right_arithmetic(local, 2) - lax.shift_right_arithmetic(i, 2),
                    (local & 3) - (i & 3),
                    local,
                )

            return counts[0] + later, counts[1] + over

        return lax.fori_loop(0, near_count[i], slot, counts)

    twice, over = lax.fori_loop(0, LEAVES, leaf_pairs, (jnp.int32(0), jnp.int32(0)))
    put(twice, 0, 0, LEAVES, 0, 0, LEAVES)
    for p in range(4):
        put(SINGLE + LEAVES + over + p, 0, 0, LEAVES, 0, 0, LEAVES)
    lists[5, 0] = (twice + 1) & -2
    lists[5, 1] = LEAVES + over
    lists[5, 2] = r


def put_sources(xy, sf, at):
    rows = source_rows(xy[0:1], xy[1:2])
    rows = jnp.concatenate([rows[:, n * QUART : (n + 1) * QUART] for n in range(4)], axis=0)
    turned = rows.T
    for n in range(4):
        sf[at + n] = turned[:, n * 32 : (n + 1) * 32].astype(B)


def weights(c):
    high = c.astype(B).astype(F)
    return jnp.concatenate([high, c - high], axis=0).astype(B)


def near_kernel(w, n_carried, *refs):
    refs = list(refs)

    def take(n):
        taken = refs[:n]
        del refs[:n]
        return taken

    last = w == WINDOWS - 1
    lists, coords, tab, sf = take(4)
    if w == 0:
        own, first, second, place = take(4)
    else:
        cw, call_w, acc_in, quart_in = take(4)
    if w == WINDOWS - 2:
        halos = take(2)
    carried = take(n_carried)
    outs = take(4 if last else 2)
    if w == 0:
        cw, call_w, payload = take(3)
    if w == WINDOWS - 2:
        sf_own, cw_own = sf, cw
        sf, cw = take(2)
    for ref, out in zip(carried, take(n_carried)):
        out[...] = ref[...]
    kh_a, kl_a, kh_b, kl_b = take(4)
    acc, quart = take(2) if last else outs
    r = lists[5, 2]
    mine = pl.ds(pl.multiple_of(r * QUART, QUART), QUART)

    if w == 0:
        for j in range(LEAVES):
            at = slice(j * PTS, (j + 1) * PTS)
            call_w[j] = weights(jnp.concatenate([own[:, at], first[:, at], second[:, at]], axis=0))
            cw[j] = call_w[j, :, mine]
        payload[...] = jnp.zeros_like(payload)
        for end, start in enumerate((0, 12)):
            for m in range(8):
                top = end * EDGE + 16 * m
                at = (start + m // 2) * QUART + m % 2 * 128
                payload[top : top + 2] = place[:, at : at + 128]
                at = r * QUART + (start + m // 2) * PTS + m % 2 * 128
                source = pl.ds(pl.multiple_of(at, 128), 128)
                payload[top + 2 : top + 4] = own[:, source]
                payload[top + 4 : top + 6] = first[:, source]
                payload[top + 6 : top + 10] = second[:, source]
        acc[...] = jnp.zeros_like(acc)
        quart[...] = jnp.zeros_like(quart)
    else:
        acc[...] = acc_in[...]
        quart[...] = quart_in[...]
    if w == WINDOWS - 2:
        sf[0:LEAVES] = sf_own[...]
        cw[0:LEAVES] = cw_own[...]
        for n, halo in enumerate(halos):
            halo = jnp.concatenate([halo[16 * m : 16 * m + 10] for m in range(8)], axis=1)
            put_sources(halo[0:2] - 0.5, sf, LEAVES + 4 * n)
            for j in range(4):
                cw[LEAVES + 4 * n + j] = weights(halo[2:10, j * QUART : (j + 1) * QUART])

    n_twice, n_single = lists[5, 0], lists[5, 1]

    def bounds(n):
        if n == 0:
            return jnp.int32(0), jnp.int32(0)
        if n == WINDOWS:
            return n_twice, n_single
        at = lax.div((3 * n_twice + 2 * n_single) * n, WINDOWS)
        here = n_single if n > WINDOWS - 2 else LEAVES
        single = jnp.maximum(lax.shift_right_arithmetic(at - 3 * n_twice, 1), 0)
        return jnp.minimum(n_twice, lax.div(at, 3)) & -2, jnp.minimum(here, single) & -2

    (twice_0, single_0), (twice_1, single_1) = bounds(w), bounds(w + 1)

    row = lax.broadcasted_iota(jnp.int32, (8, PTS), 0)
    low, middle = row < 3, (row >= 3) & (row < 6)
    ones = jnp.where(middle, 1.0, 0.0)

    def evaluate(p, kh, kl):
        i, j = lists[0, p], lists[1, p]
        ox, oy = lists[3, p].astype(F), lists[4, p].astype(F)
        xy = coords[:, pl.ds(pl.multiple_of(i * PTS, PTS), PTS)] - 0.5
        x = jnp.broadcast_to(xy[0:1], (8, PTS)) - ox
        y = jnp.broadcast_to(xy[1:2], (8, PTS)) - oy
        ls = limbs(x * x + y * y)
        squares = pick(row, ls, ones)
        offsets = jnp.where(low, -ox, jnp.where(middle, -oy, 0.0))
        t_rows = jnp.concatenate(
            [tab[i], jnp.concatenate([squares, offsets], axis=0).astype(B)], axis=0
        )
        s_rows = sf[j]
        for c in range(4):
            lanes = slice(c * 256, (c + 1) * 256)
            dist2 = dot(s_rows, t_rows[:, lanes], NN)
            for g in range(16):
                at = slice(g * 16, (g + 1) * 16)
                d2 = jnp.maximum(dist2[at], 1e-35)
                k = jnp.exp2((d2 * lax.rsqrt(d2)) * RATE)
                high = k.astype(B)
                kh[at, lanes] = high
                kl[at, lanes] = (k - high.astype(F)).astype(B)

    def multiply(p, kh, kl, both, none=False):
        i, j = lists[0, p], lists[1, p]
        high, low_part = kh[...], kl[...]
        to = jnp.where(none, LEAVES, lists[2, p])
        acc[to] += dot(cw[j], high, NN) + dot(cw[j], low_part, NN)
        if both:
            to = jnp.where(none, LEAVES, lists[6, p])
            quart[to] += dot(call_w[i], high, NT) + dot(call_w[i], low_part, NT)

    def run(begin, end, both):
        def step(n, _):
            p = begin + 2 * n
            evaluate(p, kh_a, kl_a)
            multiply(jnp.maximum(p - 1, begin), kh_b, kl_b, both, n == 0)
            evaluate(p + 1, kh_b, kl_b)
            multiply(p, kh_a, kl_a, both)
            return 0

        steps = (end - begin + 1) // 2

        @pl.when(steps > 0)
        def _():
            lax.fori_loop(0, steps, step, 0)
            multiply(begin + 2 * steps - 1, kh_b, kl_b, both)

    run(twice_0, twice_1, True)
    run(single_0 + SINGLE, single_1 + SINGLE, False)

    if last:
        for i in range(LEAVES):
            v = (acc[i, 0:8, :] + acc[i, 8:16, :]) * (PTS**-0.5)
            for k in range(RHS):
                outs[k][:, i * PTS : (i + 1) * PTS] = v[2 * k : 2 * k + 2]
            q = (quart[i, 0:8, :] + quart[i, 8:16, :]) * (PTS**-0.5)
            at = pl.ds(pl.multiple_of(r * QUART + i * PTS, QUART), QUART)
            for k in range(RHS):
                outs[k][:, at] += q[2 * k : 2 * k + 2]


def bf16(*shape):
    return jax.ShapeDtypeStruct(shape, B)


def split_rows(v):
    high = v.astype(B).astype(F)
    return jnp.concatenate([high, v - high], axis=0).astype(B)


def split_dot(rows, matrix, dims):
    high = matrix.astype(B)
    low = (matrix - high.astype(F)).astype(B)
    v = dot(rows, high, dims) + dot(rows, low, dims)
    return v[0:8] + v[8:16]


def up_kernel(charges, basis, transfer, out):
    row = lax.broadcasted_iota(jnp.int32, (8, PTS), 0)

    def put(at, v):
        out[at : at + 1, 0:RANK] = v[0:1]
        out[at : at + 1, RANK : 2 * RANK] = v[1:2]

    current = []
    for i in range(LEAVES):
        c = charges[:, i * PTS : (i + 1) * PTS]
        c = jnp.where(row == 0, c[0:1], jnp.where(row == 1, c[1:2], 0.0))
        v = split_dot(split_rows(c), basis[i], NT)
        put(i, v)
        current.append(v)
    for level in range(1, 5):
        per_block = 8 >> (level - 1)
        lifted = [
            dot_hi(v, transfer[d // per_block, TRANSFER_OFFSETS[level - 1] + d % per_block], NN)
            for d, v in enumerate(current)
        ]
        current = [lifted[d] + lifted[d + 1] for d in range(0, len(lifted), 2)]
        for d, v in enumerate(current):
            put(LEVEL_ROW[level] + d, v)
    out[31:32, :] = jnp.zeros((1, 2 * RANK), F)


def couple(block, rows, table, coupling, picked, products):
    picked[120:128, :] = jnp.zeros((8, 2 * RANK), F)
    for q in range(PAIRS):
        picked[q : q + 1, :] = table[pl.ds(rows[block, q], 1), :]
    turned = picked[...].T
    g = [turned[c * RANK : (c + 1) * RANK, 0:PAIRS] for c in range(2)]

    def part(n, _):
        at = pl.ds(pl.multiple_of(n * 8, 8), 8)
        b = coupling[block, at]
        for c in range(2):
            products[c, at, :] = jnp.sum(b * g[c][None], axis=1)
        return 0

    lax.fori_loop(0, RANK // 8, part, 0)
    pair = lax.broadcasted_iota(jnp.int32, (16, PAIRS), 1)
    target = lax.broadcasted_iota(jnp.int32, (16, PAIRS), 0)
    member = jnp.where(lax.shift_right_arithmetic(pair, 3) == target, 1.0, 0.0)
    return [dot_hi(member, products[c], NT) for c in range(2)]


def down_kernel(rows, own, other, coupling, transfer, basis, out, table, picked, products, held):
    half = own.shape[0]
    table[0:half, :] = own[...]
    table[half : 2 * half, :] = other[...]
    held[...] = jnp.zeros_like(held)
    for block in range(2):
        for c, t in enumerate(couple(block, rows, table, coupling, picked.at[block], products.at[block])):
            for n in range(16):
                held[16 * block + n, c : c + 1, :] = t[n : n + 1]
    current = [held[15] + held[31]]
    first = (0, 8, 12, 14)
    for level in range(4, 0, -1):
        per_block = 8 >> (level - 1)
        current = [
            held[16 * (d // per_block) + first[level - 1] + d % per_block]
            + dot_hi(
                current[d // 2],
                transfer[d // per_block, TRANSFER_OFFSETS[level - 1] + d % per_block],
                NT,
            )
            for d in range(2 * per_block)
        ]
    for i in range(LEAVES):
        v = split_dot(split_rows(current[i]), basis[i], NN)
        out[:, i * PTS : (i + 1) * PTS] = v[0:2]


def shards(coords, charges, leaf_basis, transfer, coupling, far_pairs, near_list, near_count):
    device = lax.axis_index("leaf").astype(jnp.int32)
    rhs_index = lax.axis_index("rhs").astype(jnp.int32)
    meta = jnp.stack([device * LEAVES, rhs_index])
    count = NX * NZ * NC

    def swap_rhs(v, k):
        return lax.ppermute(v, "rhs", [(i, i ^ k) for i in range(RHS)])

    def shift_leaf(v, s):
        pairs = [(d, (d + s) % count if s else d ^ SWAP) for d in range(count)]
        return lax.ppermute(v, "leaf", pairs)

    first = swap_rhs(charges, 1)
    onward = jnp.concatenate([charges, first], 0)
    (table,) = call(up_kernel, [(32, 2 * RANK)], [VMEM] * 3, micros=4)(
        charges, leaf_basis, transfer
    )
    lists, sf, tab, place, table = call(
        prep_kernel,
        [
            jax.ShapeDtypeStruct((8, 128), jnp.int32),
            bf16(LEAVES, QUART, 32),
            bf16(LEAVES, 16, PTS),
            (2, LEAVES * QUART),
            (32, 2 * RANK),
        ],
        [SMEM, HBM, HBM, VMEM, ANY, VMEM],
        [
            pltpu.SMEM((LEAVES, NEAR), jnp.int32),
            pltpu.SMEM((LEAVES,), jnp.int32),
            pltpu.SemaphoreType.DMA((2,)),
        ],
        micros=4,
        smem_outs=1,
    )(meta, near_list, near_count, coords, onward, table)
    second = swap_rhs(onward, 2)
    acc_shape, quart_shape = (LEAVES + 1, 16, PTS), (LEAVES + 1, 16, QUART)
    values = [pltpu.VMEM((QUART, PTS), B)] * 4
    after, edges = table, None
    for w, s in enumerate(SHIFTS):
        rows = after.shape[0]
        got = shift_leaf(after if edges is None else jnp.concatenate([after, edges], 0), s)
        if w == 1:
            up, edges = got[rows : rows + EDGE], got[rows + EDGE :]
        if w == 2:
            down, edges = got[rows:], None
        data, extra, scratch = [lists, coords, tab, sf], [], [*values]
        if w == 0:
            data += [charges, first, second, place]
            extra = [bf16(LEAVES, 16, QUART), bf16(LEAVES, 16, PTS), (2 * EDGE, 128)]
        else:
            data += [cw, call_w, acc, quart]
        if w == WINDOWS - 1:
            scratch += [pltpu.VMEM(acc_shape, F), pltpu.VMEM(quart_shape, F)]
        if w == WINDOWS - 2:
            data += [down, up]
            extra = [bf16(24, QUART, 32), bf16(24, 16, QUART)]
        carried = [after] if w < WINDOWS - 1 else []
        outs = [(2, LEAVES * PTS)] * 4 if w == WINDOWS - 1 else [acc_shape, quart_shape]
        result = call(
            functools.partial(near_kernel, w, len(carried)),
            [*outs, *extra, *(v.shape for v in carried)],
            [SMEM] + [VMEM] * (len(data) + len(carried) - 1),
            scratch,
            micros=9,
        )(*data, *carried)
        if w == WINDOWS - 1:
            whole = result
            break
        acc, quart = result[:2]
        after = jnp.concatenate([result[-1], got[:rows]], 0)
        if w == 0:
            cw, call_w, edges = result[2:5]
        if w == WINDOWS - 2:
            sf, cw = result[2:4]
    other = got

    level = jnp.asarray([k for k in range(5) for _ in range(64 >> k)], jnp.int32)[None, :]
    owner = lax.shift_right_logical(far_pairs, 4 - level)
    inside = far_pairs & (lax.shift_left(jnp.int32(1), 4 - level) - 1)
    start = jnp.asarray([LEVEL_ROW[k] for k in range(5) for _ in range(64 >> k)], jnp.int32)[None, :]
    bit_0 = lax.shift_right_logical(owner - device + 2, 3) & 1
    place_on = ((owner ^ (SWAP * bit_0)) - device) & (count - 1)
    bit_1 = place_on & 1
    half = lax.shift_right_logical(place_on, 1)
    bit_2 = half & 1
    fourth = lax.shift_right_logical(half + bit_2, 1)
    bit_3, bit_5, bit_4 = (lax.shift_right_logical(fourth, n) & 1 for n in (0, 2, 3))
    block = bit_0 + 2 * bit_1 + 4 * bit_2 + 8 * bit_3 + 16 * bit_4 + 32 * bit_5
    rows = block * 32 + start + inside
    back = [swap_rhs(whole[k], k) for k in (2, 1, 3)]
    (distant,) = call(
        down_kernel,
        [(2, LEAVES * PTS)],
        [SMEM] + [VMEM] * 5,
        [
            pltpu.VMEM((2048, 2 * RANK), F),
            pltpu.VMEM((2, 128, 2 * RANK), F),
            pltpu.VMEM((2, 2, RANK, PAIRS), F),
            pltpu.VMEM((32, 8, RANK), F),
        ],
        micros=8,
    )(rows, after, other, coupling.transpose(0, 2, 3, 1), transfer, leaf_basis)
    return distant + whole[0] + back[0] + back[1] + back[2]


def solution(mesh):
    return jax.shard_map(
        shards,
        mesh=mesh,
        in_specs=(
            P(None, "leaf"),
            P("rhs", "leaf"),
            P("leaf", None, None),
            P("leaf", None, None, None),
            P("leaf", None, None, None),
            P("leaf", None),
            P("leaf", None),
            P("leaf"),
        ),
        out_specs=P("rhs", "leaf"),
        check_vma=False,
    )
```
